128 devices in a mesh: kx: 8 (over y_hi, z), ky: 16 (over y_lo, x, core).
Axes of the slice: x: 4, y: 4 (y_hi: 2, y_lo: 2; y = y_hi * 2 + y_lo), z: 4, core: 2. Of those that a mesh axis runs over, the one named last changes fastest.
Arguments:
- green: bfloat16 [2, 512, 512, 256], P(None, 'kx', 'ky'), may hold values from -6 to 6
- vertex: bfloat16 [2, 12, 256, 256], replicated, may hold values from -0.078125 to 0.078125
Outputs:
- sigma: float32 [2, 512, 512, 256], P(None, 'kx', 'ky')
The draws below stay inside these ranges and needn't reach their ends.
All inputs are finite; a program needn't handle non-finite values.
Results may differ from the reference program's by a relative error of at most 0.04.
Values may be sent and summed in bfloat16 or wider, within the bound.
No kernel may reach another device: no remote copies, remote signals or barrier semaphores. Data moves between devices by JAX's collectives and lax.ppermute only.
A program may use at most 128 MiB of HBM per device.

```python
import jax
import jax.numpy as jnp
from jax import lax

L = 512
NF = 256
NB = 12


def block_scale(stream_key, shape, split, smallest, largest):
    def one(axis_at, parts):
        draws = jax.random.uniform(jax.random.fold_in(jax.random.fold_in(stream_key, 6), axis_at), (parts,), jnp.float32, smallest / len(split), largest / len(split))
        return jnp.repeat(jnp.exp(draws), shape[axis_at] // parts).reshape((-1,) + (1,) * (len(shape) - axis_at - 1))

    loudness = one(*split[0])
    for cut in split[1:]:
        loudness = loudness * one(*cut)
    return loudness


def scatter_about(rng, dims, spread, bound, pieces=(), held_as=jnp.bfloat16):
    drawn = jax.random.normal(rng, dims, jnp.float32) * spread
    if len(pieces) > 0:
        drawn = block_scale(rng, dims, pieces, -0.22, 0.18) * drawn
    return jnp.clip(drawn, min=-bound, max=bound).astype(held_as)


def setup_inputs(seed: int = 0) -> dict:
    key_of = jax.random.split(jax.random.key(seed), 3)
    green = scatter_about(key_of[0], (2, L, L, NF), 1.0, 6.0, ((1, 8), (2, 16)))
    vertex = scatter_about(key_of[1], (2, NB, NF, NF), (2 * NF * NB) ** -0.5, 0.078125)
    return {"green": green, "vertex": vertex}


def flip_back(values, along_axis):
    return jnp.roll(jnp.flip(values, along_axis), 1, along_axis)


def contract(rows_green, rows_mirror, vertex):
    freqs = rows_green.shape[2]
    bosons = vertex.shape[1]
    padding = ((0, 0), (0, 0), (0, bosons))
    padded_green = jnp.pad(rows_green, padding)
    padded_mirror = jnp.pad(rows_mirror, padding)

    def advance(carry, boson):
        acc_re, acc_im = carry
        left_re = rows_green[0].astype(jnp.float32)
        left_im = rows_green[1].astype(jnp.float32)
        shift_m = lax.dynamic_slice_in_dim(padded_mirror, boson, freqs, 2).astype(jnp.float32)
        shift_g = lax.dynamic_slice_in_dim(padded_green, boson, freqs, 2).astype(jnp.float32)
        bubble_re = (left_re * shift_m[0] - left_im * shift_m[1]).astype(jnp.bfloat16)
        bubble_im = (left_re * shift_m[1] + left_im * shift_m[0]).astype(jnp.bfloat16)
        panel_re = vertex[0, boson].T
        panel_im = vertex[1, boson].T
        block = jnp.concatenate([jnp.concatenate([panel_re, panel_im], 1), jnp.concatenate([-panel_im, panel_re], 1)], 0)
        joined = jnp.concatenate([bubble_re, bubble_im], 1)
        product = jnp.dot(joined, block, preferred_element_type=jnp.float32)
        cross_re = product[:, :freqs]
        cross_im = product[:, freqs:]
        acc_re = acc_re + shift_g[0] * cross_re - shift_g[1] * cross_im
        acc_im = acc_im + shift_g[0] * cross_im + shift_g[1] * cross_re
        return (acc_re, acc_im), None

    zeros = jnp.zeros((rows_green.shape[1], freqs), jnp.float32)
    totals, unused = lax.scan(advance, (zeros, zeros), jnp.arange(bosons, dtype=jnp.int32))
    return totals


def reference(green, vertex):
    momentum = lax.complex(green[0].astype(jnp.float32), green[1].astype(jnp.float32))
    half = jnp.fft.ifft(momentum, axis=1) * L
    half_re = half.real.astype(jnp.bfloat16)
    half_im = half.imag.astype(jnp.bfloat16)
    half = lax.complex(half_re.astype(jnp.float32), half_im.astype(jnp.float32))
    lattice = jnp.fft.ifft(half, axis=0)
    pair = jnp.stack([lattice.real, lattice.imag]).astype(jnp.bfloat16)
    mirror_pair = flip_back(flip_back(pair, 1), 2)
    acc_re, acc_im = contract(pair.reshape(2, L * L, NF), mirror_pair.reshape(2, L * L, NF), vertex)
    field = lax.complex(acc_re, acc_im).reshape(L, L, NF)
    result = jnp.fft.fft(jnp.fft.fft(field, axis=0), axis=1) / L
    return jnp.stack([result.real, result.imag]).astype(jnp.float32)
```

```python
import math

import jax
import jax.numpy as jnp
import ml_dtypes
import numpy as np
from jax import lax
from jax.experimental import pallas as pl
from jax.experimental.pallas import tpu as pltpu
from jax.sharding import PartitionSpec as P

LANES = 128
ROWS = 256


def pair_list(length):
    half = length // 2
    upper = (length - np.arange(half)) % length
    upper[0] = half
    return np.concatenate([np.arange(half), upper])


def complex_table(sites, momenta, length, direction, scale):
    phase = (sites[:, None].astype(np.int64) * momenta[None, :] % length) * (
        direction * 2.0 * math.pi / length
    )
    cos, sin = np.cos(phase) * scale, np.sin(phase) * scale
    return np.stack([np.stack([cos, -sin], 1), np.stack([sin, cos], 1)], 0)


def tables(length, groups):
    quad = length // groups
    half_quad = quad // 2
    pairs = pair_list(length)
    natural = np.arange(length)
    own = np.stack(
        [pairs[: length // 2].reshape(groups, half_quad), pairs[length // 2 :].reshape(groups, half_quad)], 1
    ).reshape(groups, quad)
    n = 2 * length
    t_y = complex_table(own.T.reshape(-1), natural, length, 1.0, 1.0)
    t_y = t_y.reshape(2, quad, groups, 2, length).transpose(1, 0, 2, 3, 4).reshape(n, n)
    t_x = complex_table(pairs, natural, length, 1.0, 1.0 / length)
    t_x = t_x.reshape(2, length, 2, length).transpose(0, 1, 3, 2).reshape(n, n)
    b_x = complex_table(natural, pairs, length, -1.0, 1.0)
    b_x = b_x.transpose(1, 0, 2, 3).reshape(n, n)
    b_y = complex_table(natural, own.T.reshape(-1), length, -1.0, 1.0 / length)
    b_y = b_y.reshape(2, length, 2, quad, groups).transpose(0, 1, 3, 2, 4).reshape(n, n)
    return [t.astype(ml_dtypes.bfloat16) for t in (t_y, t_x, b_x, b_y)]


def dot(left, right):
    return jnp.dot(left, right, preferred_element_type=jnp.float32)


def columns_kernel(quad, groups, freqs, block_ref, table_ref, out_ref, wide_ref):
    length = quad * groups

    def row(r, carry):
        rhs = jnp.concatenate(
            [block_ref[:, c, r].reshape(length, freqs) for c in range(2)], 0
        )
        for col in range(quad):
            for c in range(2):
                m = (col * 2 + c) * groups
                part = dot(table_ref[m : m + groups, :], rhs)
                for k in range(freqs // LANES):
                    spots = pl.ds(r * 2 + c, groups, stride=2 * quad)
                    wide_ref[col * (freqs // LANES) + k, spots, :] = part[:, k * LANES : (k + 1) * LANES]
        return carry

    lax.fori_loop(0, quad, row, 0)

    def settle(i, carry):
        at = pl.ds(pl.multiple_of(i * 128, 128), 128)
        for k in range(quad * freqs // LANES):
            out_ref[at, k * LANES : (k + 1) * LANES] = wide_ref[k, at, :].astype(jnp.bfloat16)
        return carry

    lax.fori_loop(0, 2 * length // 128, settle, 0)


def shifted(values, by):
    if by == 0:
        return values
    tail = jnp.zeros((values.shape[0], by), values.dtype)
    return jnp.concatenate([values[:, by:], tail], 1)


def sites_kernel(quad, freqs, bosons, spot_ref, block_ref, fore_ref, panel_ref, back_ref, out_ref, green_ref, field_ref):
    length = fore_ref.shape[0] // 2
    half = length // 2
    steps = half // ROWS
    first = spot_ref[0] == 0

    for col in range(quad):
        lanes = slice(col * freqs, (col + 1) * freqs)

        def lattice(i, carry):
            at = pl.ds(pl.multiple_of(i * 256, 256), 256)
            green_ref[col, at, :] = dot(fore_ref[at, :], block_ref[:, lanes]).astype(jnp.bfloat16)
            return carry

        lax.fori_loop(0, 2 * length // 256, lattice, 0)

    def site_block(step, carry):
        col = step // (2 * steps)
        side = (step // steps) % 2
        start = (step % steps) * ROWS
        partner = jnp.where(jnp.logical_and(first, col % 2 == 0), col, (col + quad // 2) % quad)
        here = side * half + start
        there = (1 - side) * half + start
        own_rows = [pl.ds(pl.multiple_of(c * length + here, ROWS), ROWS) for c in range(2)]
        far_rows = [pl.ds(pl.multiple_of(c * length + there, ROWS), ROWS) for c in range(2)]
        g_re = green_ref[col, own_rows[0], :]
        g_im = green_ref[col, own_rows[1], :]
        index = lax.broadcasted_iota(jnp.int32, (ROWS, freqs), 0) + start
        m_re = jnp.where(index == 0, green_ref[partner, own_rows[0], :], green_ref[partner, far_rows[0], :])
        m_im = jnp.where(index == 0, green_ref[partner, own_rows[1], :], green_ref[partner, far_rows[1], :])
        acc_re = jnp.zeros((ROWS, freqs), jnp.float32)
        acc_im = jnp.zeros((ROWS, freqs), jnp.float32)
        for w in range(bosons):
            s_re, s_im = shifted(m_re, w), shifted(m_im, w)
            bubble = jnp.concatenate([g_re * s_re - g_im * s_im, g_re * s_im + g_im * s_re], 1)
            cross = dot(bubble, panel_ref[w]).astype(jnp.bfloat16)
            c_re, c_im = cross[:, :freqs], cross[:, freqs:]
            h_re, h_im = shifted(g_re, w), shifted(g_im, w)
            acc_re = acc_re + (h_re * c_re - h_im * c_im).astype(jnp.float32)
            acc_im = acc_im + (h_re * c_im + h_im * c_re).astype(jnp.float32)
        field_ref[col, own_rows[0], :] = acc_re.astype(jnp.bfloat16)
        field_ref[col, own_rows[1], :] = acc_im.astype(jnp.bfloat16)
        return carry

    lax.fori_loop(0, quad * 2 * steps, site_block, 0)

    for col in range(quad):
        lanes = slice(col * freqs, (col + 1) * freqs)

        def momenta(i, carry):
            at = pl.ds(pl.multiple_of(i * 256, 256), 256)
            out_ref[at, lanes] = dot(back_ref[at, :], field_ref[col]).astype(jnp.bfloat16)
            return carry

        lax.fori_loop(0, 2 * length // 256, momenta, 0)


def rows_kernel(quad, groups, freqs, block_ref, table_ref, out_ref, wide_ref, rhs_ref):
    length = quad * groups
    targets, width = out_ref.shape[0], out_ref.shape[3]

    def widen(i, carry):
        at = pl.ds(pl.multiple_of(i * 128, 128), 128)
        for k in range(quad * freqs // LANES):
            wide_ref[k, at, :] = block_ref[at, k * LANES : (k + 1) * LANES].astype(jnp.float32)
        return carry

    lax.fori_loop(0, 2 * length // 128, widen, 0)

    def row(r, carry):
        for col in range(quad):
            for c in range(2):
                m = (col * 2 + c) * groups
                for k in range(freqs // LANES):
                    part = wide_ref[col * (freqs // LANES) + k, pl.ds(r * 2 + c, groups, stride=2 * quad), :]
                    rhs_ref[m : m + groups, k * LANES : (k + 1) * LANES] = part.astype(jnp.bfloat16)
        for c in range(2):
            for h in range(2):
                at = c * length + h * (length // 2)
                part = dot(table_ref[at : at + length // 2, :], rhs_ref[...])
                out_ref[h * (targets // 2) : (h + 1) * (targets // 2), c, r] = part.reshape(
                    targets // 2, width, freqs
                ).astype(jnp.bfloat16)
        return carry

    lax.fori_loop(0, quad, row, 0)


def in_vmem():
    return pl.BlockSpec(memory_space=pltpu.VMEM)


def call(kernel, out_shape, in_specs, scratch, flops, limit, name):
    return pl.pallas_call(
        kernel,
        out_shape=jax.ShapeDtypeStruct(out_shape, jnp.bfloat16),
        in_specs=in_specs,
        out_specs=in_vmem(),
        scratch_shapes=scratch,
        compiler_params=pltpu.CompilerParams(vmem_limit_bytes=limit * 2**20),
        cost_estimate=pl.CostEstimate(flops=flops, bytes_accessed=2**22, transcendentals=0),
        name=name,
    )


def per_device(green, vertex):
    kx, ky = lax.axis_size("kx"), lax.axis_size("ky")
    groups = kx * ky
    rows, width, freqs = green.shape[1:]
    length = width * ky
    quad = length // groups
    bosons = vertex.shape[1]
    n = 2 * length
    t_y, t_x, b_x, b_y = [jnp.asarray(t) for t in tables(length, groups)]
    both = ("kx", "ky")

    turned = jnp.swapaxes(vertex, 2, 3)
    panels = jnp.concatenate(
        [
            jnp.concatenate([turned[0], turned[1]], 2),
            jnp.concatenate([-turned[1], turned[0]], 2),
        ],
        1,
    )

    block = green.reshape(2, ky, quad, width, freqs).transpose(1, 0, 2, 3, 4)
    block = lax.all_to_all(block, "ky", split_axis=0, concat_axis=0, tiled=True)
    spectrum = call(
        lambda *refs: columns_kernel(quad, groups, freqs, *refs),
        (n, quad * freqs),
        [in_vmem()] * 2,
        [pltpu.VMEM((quad * freqs // LANES, n, LANES), jnp.float32)],
        2 * n * n * quad * freqs,
        16,
        "to_columns",
    )(block, t_y)
    spectrum = lax.all_to_all(spectrum, both, split_axis=0, concat_axis=0, tiled=True)
    spot = (lax.axis_index("kx") * ky + lax.axis_index("ky")).astype(jnp.int32).reshape(1)
    field = call(
        lambda *refs: sites_kernel(quad, freqs, bosons, *refs),
        (n, quad * freqs),
        [pl.BlockSpec(memory_space=pltpu.SMEM)] + [in_vmem()] * 4,
        [
            pltpu.VMEM((quad, n, freqs), jnp.bfloat16),
            pltpu.VMEM((quad, n, freqs), jnp.bfloat16),
        ],
        2 * n * n * quad * freqs * 2 + 8 * bosons * length * quad * freqs * freqs,
        32,
        "on_sites",
    )(spot, spectrum, t_x, panels, b_x)
    field = lax.all_to_all(field, both, split_axis=0, concat_axis=0, tiled=True)
    settled = call(
        lambda *refs: rows_kernel(quad, groups, freqs, *refs),
        (ky, 2, quad, width, freqs),
        [in_vmem()] * 2,
        [pltpu.VMEM((quad * freqs // LANES, n, LANES), jnp.float32), pltpu.VMEM((n, freqs), jnp.bfloat16)],
        2 * n * n * quad * freqs,
        16,
        "to_rows",
    )(field, b_y)
    settled = lax.all_to_all(settled, "ky", split_axis=0, concat_axis=0, tiled=True)
    return settled.transpose(1, 0, 2, 3, 4).reshape(2, rows, width, freqs).astype(jnp.float32)


def solution(mesh):
    placed = (P(None, "kx", "ky", None), P())
    return jax.shard_map(
        per_device, mesh=mesh, in_specs=placed, out_specs=P(None, "kx", "ky", None), check_vma=False
    )
```

```python
import math

import jax
import jax.numpy as jnp
import ml_dtypes
import numpy as np
from jax import lax
from jax.experimental import pallas as pl
from jax.experimental.pallas import tpu as pltpu
from jax.sharding import PartitionSpec as P

LANES = 128
TILE = 16
GROUP = 4


def pair_list(length):
    half = length // 2
    upper = (length - np.arange(half)) % length
    upper[0] = half
    return np.concatenate([np.arange(half), upper])


def complex_table(sites, momenta, length, direction, scale):
    phase = (sites[:, None].astype(np.int64) * momenta[None, :] % length) * (
        direction * 2.0 * math.pi / length
    )
    cos, sin = np.cos(phase) * scale, np.sin(phase) * scale
    return np.stack([np.stack([cos, -sin], 1), np.stack([sin, cos], 1)], 0)


def tables(length, groups):
    quad = length // groups
    half_quad = quad // 2
    pairs = pair_list(length)
    natural = np.arange(length)
    own = np.stack(
        [pairs[: length // 2].reshape(groups, half_quad), pairs[length // 2 :].reshape(groups, half_quad)], 1
    ).reshape(groups, quad)
    n = 2 * length
    t_y = complex_table(own.T.reshape(-1), natural, length, 1.0, 1.0)
    t_y = t_y.reshape(2, quad, groups, 2, length).transpose(1, 0, 2, 3, 4).reshape(n, n)
    t_x = complex_table(pairs, natural, length, 1.0, 1.0 / length)
    t_x = t_x.reshape(2, length, 2, length).transpose(0, 1, 3, 2).reshape(n, n)
    b_x = complex_table(natural, pairs, length, -1.0, 1.0)
    b_x = b_x.transpose(1, 0, 2, 3).reshape(n, n)
    b_y = complex_table(natural, own.T.reshape(-1), length, -1.0, 1.0 / length)
    b_y = b_y.reshape(2, length, 2, quad, groups).transpose(0, 1, 3, 2, 4).reshape(n, n)
    return [t.astype(ml_dtypes.bfloat16) for t in (t_y, t_x, b_x, b_y)]


def dot(left, right):
    return jnp.dot(left, right, preferred_element_type=jnp.float32)


def columns_kernel(quad, groups, freqs, block_ref, table_ref, panel_hbm, out_ref, wide_ref):
    del panel_hbm
    length = quad * groups

    def row(r, carry):
        rhs = jnp.concatenate(
            [block_ref[:, c, r].reshape(length, freqs) for c in range(2)], 0
        )
        product = dot(table_ref[...], rhs)
        for col in range(quad):
            for c in range(2):
                m = (col * 2 + c) * groups
                part = product[m : m + groups]
                for k in range(freqs // LANES):
                    spots = pl.ds(r * 2 + c, groups, stride=2 * quad)
                    wide_ref[col * (freqs // LANES) + k, spots, :] = part[:, k * LANES : (k + 1) * LANES]
        return carry

    lax.fori_loop(0, quad, row, 0)

    def settle(i, carry):
        at = pl.ds(pl.multiple_of(i * 128, 128), 128)
        for k in range(quad * freqs // LANES):
            out_ref[at, k * LANES : (k + 1) * LANES] = wide_ref[k, at, :].astype(jnp.bfloat16)
        return carry

    lax.fori_loop(0, 2 * length // 128, settle, 0)


def shifted(values, by):
    if by == 0:
        return values
    tail = jnp.zeros((values.shape[0], by), values.dtype)
    return jnp.concatenate([values[:, by:], tail], 1)


def swap_first(ref, col, c):
    low, high = ref[col, 2 * c, :TILE, :], ref[col, 2 * c + 1, :TILE, :]
    top = lax.broadcasted_iota(jnp.int32, low.shape, 0) == 0
    ref[col, 2 * c, :TILE, :] = jnp.where(top, high, low)
    ref[col, 2 * c + 1, :TILE, :] = jnp.where(top, low, high)


def sites_kernel(
    quad, freqs, bosons, spot_ref, block_ref, fore_hbm, panel_hbm, back_hbm, out_ref,
    fore_ref, panel_ref, back_ref, green_ref, field_ref, fore_sem, panel_sem, back_sem,
):
    half = green_ref.shape[2]
    first = spot_ref[0] == 0
    fore = [
        pltpu.make_async_copy(fore_hbm.at[pl.ds(i * half, half)], fore_ref.at[pl.ds(i * half, half)], fore_sem.at[i])
        for i in range(4)
    ]
    for copy in fore:
        copy.start()
    panel = pltpu.make_async_copy(panel_hbm, panel_ref, panel_sem)
    panel.start()
    back = pltpu.make_async_copy(back_hbm, back_ref, back_sem)
    back.start()

    for i in range(4):
        fore[i].wait()
        lattice = dot(fore_ref[i * half : (i + 1) * half, :], block_ref[...]).astype(jnp.bfloat16)
        for col in range(quad):
            green_ref[col, i] = lattice[:, col * freqs : (col + 1) * freqs]
    for col in range(quad // 2, quad):
        for c in range(2):
            swap_first(green_ref, col, c)
    panel.wait()

    def pair_block(step, carry):
        column, side = step // 2, step % 2
        alone = jnp.logical_and(first, column == 0)
        p_col = jnp.where(alone, side * (quad // 2), column)
        q_col = jnp.where(alone, side * (quad // 2), column + quad // 2)
        p_re, p_im = green_ref[p_col, side], green_ref[p_col, 2 + side]
        q_re, q_im = green_ref[q_col, 1 - side], green_ref[q_col, 3 - side]
        row = lax.broadcasted_iota(jnp.int32, (TILE, freqs), 0)
        own = jnp.logical_and(row == 0, alone)

        def mirror(mine, other):
            return jnp.concatenate([jnp.where(own, mine[:TILE], other[:TILE]), other[TILE:]], 0)

        totals = [jnp.zeros((half, freqs), jnp.float32) for _ in range(4)]
        for start in range(0, bosons, GROUP):
            sums = None
            for w in range(start, min(start + GROUP, bosons)):
                sp_re, sp_im = shifted(p_re, w), shifted(p_im, w)
                sq_re, sq_im = shifted(q_re, w), shifted(q_im, w)
                lefts = []
                for g_re, g_im, m_re, m_im in (
                    (p_re, p_im, mirror(sp_re, sq_re), mirror(sp_im, sq_im)),
                    (q_re, q_im, mirror(sq_re, sp_re), mirror(sq_im, sp_im)),
                ):
                    b_re = g_re * m_re - g_im * m_im
                    b_im = g_re * m_im + g_im * m_re
                    lefts += [jnp.concatenate([b_re, -b_im], 1), jnp.concatenate([b_im, b_re], 1)]
                cross = dot(jnp.concatenate(lefts, 0), panel_ref[w]).astype(jnp.bfloat16)
                cp_re, cp_im, cq_re, cq_im = [cross[i * half : (i + 1) * half] for i in range(4)]
                terms = [
                    sp_re * cp_re - sp_im * cp_im,
                    sp_re * cp_im + sp_im * cp_re,
                    sq_re * cq_re - sq_im * cq_im,
                    sq_re * cq_im + sq_im * cq_re,
                ]
                sums = terms if sums is None else [s + t for s, t in zip(sums, terms)]
            totals = [t + s.astype(jnp.float32) for t, s in zip(totals, sums)]
        p_sum_re, p_sum_im, q_sum_re, q_sum_im = [t.astype(jnp.bfloat16) for t in totals]
        field_ref[p_col, side] = p_sum_re
        field_ref[p_col, 2 + side] = p_sum_im
        field_ref[q_col, 1 - side] = q_sum_re
        field_ref[q_col, 3 - side] = q_sum_im
        return carry

    lax.fori_loop(0, quad, pair_block, 0)

    for col in range(quad // 2, quad):
        for c in range(2):
            swap_first(field_ref, col, c)
    back.wait()
    for col in range(quad):
        stacked = field_ref[col].reshape(4 * half, freqs)
        out_ref[:, col * freqs : (col + 1) * freqs] = dot(back_ref[...], stacked).astype(jnp.bfloat16)


def rows_kernel(quad, groups, freqs, block_ref, table_ref, out_ref, wide_ref, rhs_ref):
    length = quad * groups
    targets, width = out_ref.shape[0], out_ref.shape[3]

    def widen(i, carry):
        at = pl.ds(pl.multiple_of(i * 128, 128), 128)
        for k in range(quad * freqs // LANES):
            wide_ref[k, at, :] = block_ref[at, k * LANES : (k + 1) * LANES].astype(jnp.float32)
        return carry

    lax.fori_loop(0, 2 * length // 128, widen, 0)

    def row(r, carry):
        for col in range(quad):
            for c in range(2):
                m = (col * 2 + c) * groups
                for k in range(freqs // LANES):
                    part = wide_ref[col * (freqs // LANES) + k, pl.ds(r * 2 + c, groups, stride=2 * quad), :]
                    rhs_ref[m : m + groups, k * LANES : (k + 1) * LANES] = part.astype(jnp.bfloat16)
        product = dot(table_ref[...], rhs_ref[...]).astype(jnp.bfloat16)
        for c in range(2):
            part = product[c * length : (c + 1) * length]
            out_ref[:, c, r] = part.reshape(targets, width, freqs)
        return carry

    lax.fori_loop(0, quad, row, 0)


def in_vmem():
    return pl.BlockSpec(memory_space=pltpu.VMEM)


def call(kernel, out_shape, in_specs, scratch, flops, limit, name):
    return pl.pallas_call(
        kernel,
        out_shape=jax.ShapeDtypeStruct(out_shape, jnp.bfloat16),
        in_specs=in_specs,
        out_specs=in_vmem(),
        scratch_shapes=scratch,
        compiler_params=pltpu.CompilerParams(vmem_limit_bytes=limit * 2**20),
        cost_estimate=pl.CostEstimate(flops=flops, bytes_accessed=2**22, transcendentals=0),
        name=name,
    )


def per_device(green, vertex):
    kx, ky = lax.axis_size("kx"), lax.axis_size("ky")
    groups = kx * ky
    rows, width, freqs = green.shape[1:]
    length = width * ky
    quad = length // groups
    bosons = vertex.shape[1]
    n = 2 * length
    t_y, t_x, b_x, b_y = [jnp.asarray(t) for t in tables(length, groups)]
    both = ("kx", "ky")

    panels = vertex.transpose(1, 0, 3, 2).reshape(bosons, 2 * freqs, freqs)

    block = green.reshape(2, ky, quad, width, freqs).transpose(1, 0, 2, 3, 4)
    block = lax.all_to_all(block, "ky", split_axis=0, concat_axis=0, tiled=True)
    spectrum = call(
        lambda *refs: columns_kernel(quad, groups, freqs, *refs),
        (n, quad * freqs),
        [in_vmem()] * 2 + [pl.BlockSpec(memory_space=pltpu.HBM)],
        [pltpu.VMEM((quad * freqs // LANES, n, LANES), jnp.float32)],
        2 * n * n * quad * freqs,
        16,
        "to_columns",
    )(block, t_y, panels)
    spectrum = lax.all_to_all(spectrum, both, split_axis=0, concat_axis=0, tiled=True)
    spot = (lax.axis_index("kx") * ky + lax.axis_index("ky")).astype(jnp.int32).reshape(1)
    field = call(
        lambda *refs: sites_kernel(quad, freqs, bosons, *refs),
        (n, quad * freqs),
        [pl.BlockSpec(memory_space=pltpu.SMEM), in_vmem()] + [pl.BlockSpec(memory_space=pltpu.HBM)] * 3,
        [
            pltpu.VMEM((n, n), jnp.bfloat16),
            pltpu.VMEM((bosons, 2 * freqs, freqs), jnp.bfloat16),
            pltpu.VMEM((n, n), jnp.bfloat16),
            pltpu.VMEM((quad, 4, length // 2, freqs), jnp.bfloat16),
            pltpu.VMEM((quad, 4, length // 2, freqs), jnp.bfloat16),
            pltpu.SemaphoreType.DMA((4,)),
            pltpu.SemaphoreType.DMA,
            pltpu.SemaphoreType.DMA,
        ],
        2 * n * n * quad * freqs * 2 + 8 * bosons * length * quad * freqs * freqs,
        36,
        "on_sites",
    )(spot, spectrum, t_x, panels, b_x)
    field = lax.all_to_all(field, both, split_axis=0, concat_axis=0, tiled=True)
    settled = call(
        lambda *refs: rows_kernel(quad, groups, freqs, *refs),
        (ky, 2, quad, width, freqs),
        [in_vmem()] * 2,
        [pltpu.VMEM((quad * freqs // LANES, n, LANES), jnp.float32), pltpu.VMEM((n, freqs), jnp.bfloat16)],
        2 * n * n * quad * freqs,
        16,
        "to_rows",
    )(field, b_y)
    settled = lax.all_to_all(settled, "ky", split_axis=0, concat_axis=0, tiled=True)
    return settled.transpose(1, 0, 2, 3, 4).reshape(2, rows, width, freqs).astype(jnp.float32)


def solution(mesh):
    placed = (P(None, "kx", "ky", None), P())
    return jax.shard_map(
        per_device, mesh=mesh, in_specs=placed, out_specs=P(None, "kx", "ky", None), check_vma=False
    )
```

```python
import math

import jax
import jax.numpy as jnp
import ml_dtypes
import numpy as np
from jax import lax
from jax.experimental import pallas as pl
from jax.experimental.pallas import tpu as pltpu
from jax.sharding import PartitionSpec as P

LANES = 128
TILE = 16
GROUP = 4


def pair_list(length):
    half = length // 2
    upper = (length - np.arange(half)) % length
    upper[0] = half
    return np.concatenate([np.arange(half), upper])


def complex_table(sites, momenta, length, direction, scale):
    phase = (sites[:, None].astype(np.int64) * momenta[None, :] % length) * (
        direction * 2.0 * math.pi / length
    )
    cos, sin = np.cos(phase) * scale, np.sin(phase) * scale
    return np.stack([np.stack([cos, -sin], 1), np.stack([sin, cos], 1)], 0)


def tables(length, groups):
    quad = length // groups
    half_quad = quad // 2
    pairs = pair_list(length)
    natural = np.arange(length)
    own = np.stack(
        [pairs[: length // 2].reshape(groups, half_quad), pairs[length // 2 :].reshape(groups, half_quad)], 1
    ).reshape(groups, quad)
    n = 2 * length
    t_y = complex_table(own.T.reshape(-1), natural, length, 1.0, 1.0)
    t_y = t_y.reshape(2, quad, groups, 2, length).transpose(1, 0, 2, 3, 4).reshape(n, n)
    t_x = complex_table(pairs, natural, length, 1.0, 1.0 / length)
    t_x = t_x.reshape(2, length, 2, length).transpose(0, 1, 3, 2).reshape(n, n)
    b_x = complex_table(natural, pairs, length, -1.0, 1.0)
    b_x = b_x.transpose(1, 0, 2, 3).reshape(n, n)
    b_y = complex_table(natural, own.T.reshape(-1), length, -1.0, 1.0 / length)
    b_y = b_y.reshape(2, length, 2, quad, groups).transpose(0, 1, 3, 2, 4).reshape(n, n)
    return np.stack([t_y, t_x, b_x, b_y]).astype(ml_dtypes.bfloat16)


def dot(left, right):
    return jnp.dot(left, right, preferred_element_type=jnp.float32)


def dot_turned(left, right):
    return lax.dot_general(left, right, (((1,), (1,)), ((), ())), preferred_element_type=jnp.float32)


def columns_kernel(quad, groups, freqs, block_ref, table_ref, out_ref, wide_ref):
    length = quad * groups

    def row(r, carry):
        rhs = jnp.concatenate(
            [block_ref[:, c, r].reshape(length, freqs) for c in range(2)], 0
        )
        product = dot(table_ref[0], rhs)
        for col in range(quad):
            for c in range(2):
                m = (col * 2 + c) * groups
                part = product[m : m + groups]
                for k in range(freqs // LANES):
                    spots = pl.ds(r * 2 + c, groups, stride=2 * quad)
                    wide_ref[col * (freqs // LANES) + k, spots, :] = part[:, k * LANES : (k + 1) * LANES]
        return carry

    lax.fori_loop(0, quad, row, 0)

    def settle(i, carry):
        at = pl.ds(pl.multiple_of(i * 128, 128), 128)
        for k in range(quad * freqs // LANES):
            out_ref[at, k * LANES : (k + 1) * LANES] = wide_ref[k, at, :].astype(jnp.bfloat16)
        return carry

    lax.fori_loop(0, 2 * length // 128, settle, 0)


def shifted(values, by):
    if by == 0:
        return values
    tail = jnp.zeros((values.shape[0], by), values.dtype)
    return jnp.concatenate([values[:, by:], tail], 1)


def swap_first(ref, col, c):
    low, high = ref[col, 2 * c, :TILE, :], ref[col, 2 * c + 1, :TILE, :]
    top = lax.broadcasted_iota(jnp.int32, low.shape, 0) == 0
    ref[col, 2 * c, :TILE, :] = jnp.where(top, high, low)
    ref[col, 2 * c + 1, :TILE, :] = jnp.where(top, low, high)


def sites_kernel(quad, freqs, bosons, block_ref, table_ref, vertex_ref, out_ref, green_ref, field_ref):
    half = green_ref.shape[2]
    first = lax.axis_index("kx") + lax.axis_index("ky") == 0

    for i in range(4):
        lattice = dot(table_ref[1, i * half : (i + 1) * half, :], block_ref[...]).astype(jnp.bfloat16)
        for col in range(quad):
            green_ref[col, i] = lattice[:, col * freqs : (col + 1) * freqs]
    for col in range(quad // 2, quad):
        for c in range(2):
            swap_first(green_ref, col, c)

    def pair_block(step, carry):
        column, side = step // 2, step % 2
        alone = jnp.logical_and(first, column == 0)
        p_col = jnp.where(alone, side * (quad // 2), column)
        q_col = jnp.where(alone, side * (quad // 2), column + quad // 2)
        p_re, p_im = green_ref[p_col, side], green_ref[p_col, 2 + side]
        q_re, q_im = green_ref[q_col, 1 - side], green_ref[q_col, 3 - side]
        row = lax.broadcasted_iota(jnp.int32, (TILE, freqs), 0)
        own = jnp.logical_and(row == 0, alone)

        def mirror(mine, other):
            return jnp.concatenate([jnp.where(own, mine[:TILE], other[:TILE]), other[TILE:]], 0)

        totals = [jnp.zeros((half, freqs), jnp.float32) for _ in range(4)]
        for start in range(0, bosons, GROUP):
            sums = None
            for w in range(start, min(start + GROUP, bosons)):
                panel = jnp.concatenate([vertex_ref[0, w], vertex_ref[1, w]], 1)
                sp_re, sp_im = shifted(p_re, w), shifted(p_im, w)
                sq_re, sq_im = shifted(q_re, w), shifted(q_im, w)
                cross = []
                for g_re, g_im, m_re, m_im in (
                    (p_re, p_im, mirror(sp_re, sq_re), mirror(sp_im, sq_im)),
                    (q_re, q_im, mirror(sq_re, sp_re), mirror(sq_im, sp_im)),
                ):
                    b_re = g_re * m_re - g_im * m_im
                    b_im = g_re * m_im + g_im * m_re
                    for left in (jnp.concatenate([b_re, -b_im], 1), jnp.concatenate([b_im, b_re], 1)):
                        cross.append(dot_turned(left, panel).astype(jnp.bfloat16))
                cp_re, cp_im, cq_re, cq_im = cross
                terms = [
                    sp_re * cp_re - sp_im * cp_im,
                    sp_re * cp_im + sp_im * cp_re,
                    sq_re * cq_re - sq_im * cq_im,
                    sq_re * cq_im + sq_im * cq_re,
                ]
                sums = terms if sums is None else [s + t for s, t in zip(sums, terms)]
            totals = [t + s.astype(jnp.float32) for t, s in zip(totals, sums)]
        p_sum_re, p_sum_im, q_sum_re, q_sum_im = [t.astype(jnp.bfloat16) for t in totals]
        field_ref[p_col, side] = p_sum_re
        field_ref[p_col, 2 + side] = p_sum_im
        field_ref[q_col, 1 - side] = q_sum_re
        field_ref[q_col, 3 - side] = q_sum_im
        return carry

    lax.fori_loop(0, quad, pair_block, 0)

    for col in range(quad // 2, quad):
        for c in range(2):
            swap_first(field_ref, col, c)
    for col in range(quad):
        stacked = field_ref[col].reshape(4 * half, freqs)
        out_ref[:, col * freqs : (col + 1) * freqs] = dot(table_ref[2], stacked).astype(jnp.bfloat16)


def rows_kernel(quad, groups, freqs, block_ref, table_ref, out_ref, wide_ref, rhs_ref):
    length = quad * groups
    targets, width = out_ref.shape[0], out_ref.shape[3]

    def widen(i, carry):
        at = pl.ds(pl.multiple_of(i * 128, 128), 128)
        for k in range(quad * freqs // LANES):
            wide_ref[k, at, :] = block_ref[at, k * LANES : (k + 1) * LANES].astype(jnp.float32)
        return carry

    lax.fori_loop(0, 2 * length // 128, widen, 0)

    def row(r, carry):
        for col in range(quad):
            for c in range(2):
                m = (col * 2 + c) * groups
                for k in range(freqs // LANES):
                    part = wide_ref[col * (freqs // LANES) + k, pl.ds(r * 2 + c, groups, stride=2 * quad), :]
                    rhs_ref[m : m + groups, k * LANES : (k + 1) * LANES] = part.astype(jnp.bfloat16)
        product = dot(table_ref[3], rhs_ref[...]).astype(jnp.bfloat16)
        for c in range(2):
            part = product[c * length : (c + 1) * length]
            out_ref[:, c, r] = part.reshape(targets, width, freqs)
        return carry

    lax.fori_loop(0, quad, row, 0)


def in_vmem():
    return pl.BlockSpec(memory_space=pltpu.VMEM)


def call(kernel, out_shape, in_specs, scratch, flops, limit, name):
    return pl.pallas_call(
        kernel,
        out_shape=jax.ShapeDtypeStruct(out_shape, jnp.bfloat16),
        in_specs=in_specs,
        out_specs=in_vmem(),
        scratch_shapes=scratch,
        compiler_params=pltpu.CompilerParams(vmem_limit_bytes=limit * 2**20),
        cost_estimate=pl.CostEstimate(flops=flops, bytes_accessed=2**22, transcendentals=0),
        name=name,
    )


def per_device(green, vertex):
    kx, ky = lax.axis_size("kx"), lax.axis_size("ky")
    groups = kx * ky
    rows, width, freqs = green.shape[1:]
    length = width * ky
    quad = length // groups
    bosons = vertex.shape[1]
    n = 2 * length
    dfts = jnp.asarray(tables(length, groups))
    both = ("kx", "ky")

    block = green.reshape(2, ky, quad, width, freqs).transpose(1, 0, 2, 3, 4)
    block = lax.all_to_all(block, "ky", split_axis=0, concat_axis=0, tiled=True)
    spectrum = call(
        lambda *refs: columns_kernel(quad, groups, freqs, *refs),
        (n, quad * freqs),
        [in_vmem()] * 2,
        [pltpu.VMEM((quad * freqs // LANES, n, LANES), jnp.float32)],
        2 * n * n * quad * freqs,
        16,
        "to_columns",
    )(block, dfts)
    spectrum = lax.all_to_all(spectrum, both, split_axis=0, concat_axis=0, tiled=True)
    field = call(
        lambda *refs: sites_kernel(quad, freqs, bosons, *refs),
        (n, quad * freqs),
        [in_vmem()] * 3,
        [pltpu.VMEM((quad, 4, length // 2, freqs), jnp.bfloat16)] * 2,
        2 * n * n * quad * freqs * 2 + 8 * bosons * length * quad * freqs * freqs,
        24,
        "on_sites",
    )(spectrum, dfts, vertex)
    field = lax.all_to_all(field, both, split_axis=0, concat_axis=0, tiled=True)
    settled = call(
        lambda *refs: rows_kernel(quad, groups, freqs, *refs),
        (ky, 2, quad, width, freqs),
        [in_vmem()] * 2,
        [pltpu.VMEM((quad * freqs // LANES, n, LANES), jnp.float32), pltpu.VMEM((n, freqs), jnp.bfloat16)],
        2 * n * n * quad * freqs,
        16,
        "to_rows",
    )(field, dfts)
    settled = lax.all_to_all(settled, "ky", split_axis=0, concat_axis=0, tiled=True)
    return settled.transpose(1, 0, 2, 3, 4).reshape(2, rows, width, freqs).astype(jnp.float32)


def solution(mesh):
    placed = (P(None, "kx", "ky", None), P())
    return jax.shard_map(
        per_device, mesh=mesh, in_specs=placed, out_specs=P(None, "kx", "ky", None), check_vma=False
    )
```

```python
import math

import jax
import jax.numpy as jnp
import ml_dtypes
import numpy as np
from jax import lax
from jax.experimental import pallas as pl
from jax.experimental.pallas import tpu as pltpu
from jax.sharding import PartitionSpec as P

LANES = 128
TILE = 16
GROUP = 4


def pair_list(length):
    half = length // 2
    upper = (length - np.arange(half)) % length
    upper[0] = half
    return np.concatenate([np.arange(half), upper])


def complex_table(sites, momenta, length, direction, scale):
    phase = (sites[:, None].astype(np.int64) * momenta[None, :] % length) * (
        direction * 2.0 * math.pi / length
    )
    cos, sin = np.cos(phase) * scale, np.sin(phase) * scale
    return np.stack([np.stack([cos, -sin], 1), np.stack([sin, cos], 1)], 0)


def tables(length, groups):
    quad = length // groups
    half = length // 2
    pairs = pair_list(length)
    low = np.arange(half)
    own = np.stack([pairs[:half].reshape(groups, -1), pairs[half:].reshape(groups, -1)], 1).reshape(groups, quad)
    found = []
    for parity in range(2):
        y = own[:, parity::2].T.reshape(-1)
        x = np.concatenate([pairs[:half][parity::2], pairs[half:][parity::2]])
        cols = quad // 2
        t_y = complex_table(y, low, length, 1.0, 1.0)
        t_y = t_y.reshape(2, cols, groups, 2, half).transpose(1, 0, 2, 3, 4)
        t_x = complex_table(x, low, length, 1.0, 1.0 / length).transpose(0, 1, 3, 2)
        b_x = complex_table(low, x, length, -1.0, 1.0).transpose(1, 0, 2, 3)
        b_y = complex_table(low, y, length, -1.0, 1.0 / length)
        b_y = b_y.reshape(2, half, 2, cols, groups).transpose(0, 1, 3, 2, 4)
        found.append([t.reshape(length, length) for t in (t_y, t_x, b_x, b_y)])
    return np.stack([np.stack(f) for f in found], 1).astype(ml_dtypes.bfloat16)


def dot(left, right):
    return jnp.dot(left, right, preferred_element_type=jnp.float32)


def dot_turned(left, right):
    return lax.dot_general(left, right, (((1,), (1,)), ((), ())), preferred_element_type=jnp.float32)


def columns_kernel(quad, groups, freqs, block_ref, table_ref, out_ref, wide_ref):
    length = quad * groups

    def row(r, carry):
        both = [block_ref[:, c, r].reshape(length, freqs) for c in range(2)]
        low, high = [b[: length // 2] for b in both], [b[length // 2 :] for b in both]
        for parity in range(2):
            rhs = jnp.concatenate([a - b if parity else a + b for a, b in zip(low, high)], 0)
            product = dot(table_ref[0, parity], rhs)
            for at in range(quad):
                col, c = 2 * (at // 2) + parity, at % 2
                part = product[at * groups : (at + 1) * groups]
                for k in range(freqs // LANES):
                    spots = pl.ds(r * 2 + c, groups, stride=2 * quad)
                    wide_ref[col * (freqs // LANES) + k, spots, :] = part[:, k * LANES : (k + 1) * LANES]
        return carry

    lax.fori_loop(0, quad, row, 0)

    def settle(i, carry):
        at = pl.ds(pl.multiple_of(i * 128, 128), 128)
        for k in range(quad * freqs // LANES):
            out_ref[at, k * LANES : (k + 1) * LANES] = wide_ref[k, at, :].astype(jnp.bfloat16)
        return carry

    lax.fori_loop(0, 2 * length // 128, settle, 0)


def shifted(values, by):
    if by == 0:
        return values
    tail = jnp.zeros((values.shape[0], by), values.dtype)
    return jnp.concatenate([values[:, by:], tail], 1)


def swap_first(ref, col, c):
    low, high = ref[col, 2 * c, :TILE, :], ref[col, 2 * c + 1, :TILE, :]
    top = lax.broadcasted_iota(jnp.int32, low.shape, 0) == 0
    ref[col, 2 * c, :TILE, :] = jnp.where(top, high, low)
    ref[col, 2 * c + 1, :TILE, :] = jnp.where(top, low, high)


def sites_kernel(quad, freqs, bosons, block_ref, table_ref, vertex_ref, out_ref, green_ref, field_ref, mixed_ref):
    half = green_ref.shape[2]
    length = 2 * half
    part = half // 2
    first = lax.axis_index("kx") + lax.axis_index("ky") == 0

    low, high = block_ref[:length, :], block_ref[length:, :]
    for parity in range(2):
        lattice = dot(table_ref[1, parity], low - high if parity else low + high).astype(jnp.bfloat16)
        for at in range(4):
            for col in range(quad):
                green_ref[col, at, parity * part : (parity + 1) * part, :] = lattice[
                    at * part : (at + 1) * part, col * freqs : (col + 1) * freqs
                ]
    for col in range(quad // 2, quad):
        for c in range(2):
            swap_first(green_ref, col, c)
    for w in range(bosons):
        v_re, v_im = vertex_ref[0, w], vertex_ref[1, w]
        mixed_ref[0, w] = v_im - v_re
        mixed_ref[1, w] = v_re + v_im

    def pair_block(step, carry):
        column, side = step // 2, step % 2
        alone = jnp.logical_and(first, column == 0)
        p_col = jnp.where(alone, side * (quad // 2), column)
        q_col = jnp.where(alone, side * (quad // 2), column + quad // 2)
        p_re, p_im = green_ref[p_col, side], green_ref[p_col, 2 + side]
        q_re, q_im = green_ref[q_col, 1 - side], green_ref[q_col, 3 - side]
        row = lax.broadcasted_iota(jnp.int32, (TILE, freqs), 0)
        own = jnp.logical_and(row == 0, alone)

        def mirror(mine, other):
            return jnp.concatenate([jnp.where(own, mine[:TILE], other[:TILE]), other[TILE:]], 0)

        totals = [jnp.zeros((half, freqs), jnp.float32) for _ in range(4)]
        for start in range(0, bosons, GROUP):
            sums = None
            for w in range(start, min(start + GROUP, bosons)):
                sp_re, sp_im = shifted(p_re, w), shifted(p_im, w)
                sq_re, sq_im = shifted(q_re, w), shifted(q_im, w)
                b_re, b_im = [], []
                for g_re, g_im, m_re, m_im in (
                    (p_re, p_im, mirror(sp_re, sq_re), mirror(sp_im, sq_im)),
                    (q_re, q_im, mirror(sq_re, sp_re), mirror(sq_im, sp_im)),
                ):
                    b_re.append(g_re * m_re - g_im * m_im)
                    b_im.append(g_re * m_im + g_im * m_re)
                b_re, b_im = jnp.concatenate(b_re, 0), jnp.concatenate(b_im, 0)
                shared = dot_turned(b_re + b_im, vertex_ref[0, w])
                c_re = (shared - dot_turned(b_im, mixed_ref[1, w])).astype(jnp.bfloat16)
                c_im = (shared + dot_turned(b_re, mixed_ref[0, w])).astype(jnp.bfloat16)
                cp_re, cq_re, cp_im, cq_im = c_re[:half], c_re[half:], c_im[:half], c_im[half:]
                terms = [
                    sp_re * cp_re - sp_im * cp_im,
                    sp_re * cp_im + sp_im * cp_re,
                    sq_re * cq_re - sq_im * cq_im,
                    sq_re * cq_im + sq_im * cq_re,
                ]
                sums = terms if sums is None else [s + t for s, t in zip(sums, terms)]
            totals = [t + s.astype(jnp.float32) for t, s in zip(totals, sums)]
        p_sum_re, p_sum_im, q_sum_re, q_sum_im = [t.astype(jnp.bfloat16) for t in totals]
        field_ref[p_col, side] = p_sum_re
        field_ref[p_col, 2 + side] = p_sum_im
        field_ref[q_col, 1 - side] = q_sum_re
        field_ref[q_col, 3 - side] = q_sum_im
        return carry

    lax.fori_loop(0, quad, pair_block, 0)

    for col in range(quad // 2, quad):
        for c in range(2):
            swap_first(field_ref, col, c)
    for col in range(quad):
        lanes = slice(col * freqs, (col + 1) * freqs)
        even, odd = [
            dot(
                table_ref[2, parity],
                field_ref[col, :, parity * part : (parity + 1) * part, :].reshape(length, freqs),
            )
            for parity in range(2)
        ]
        out_ref[:length, lanes] = (even + odd).astype(jnp.bfloat16)
        out_ref[length:, lanes] = (even - odd).astype(jnp.bfloat16)


def rows_kernel(quad, groups, freqs, block_ref, table_ref, out_ref, wide_ref, rhs_ref):
    length = quad * groups
    targets, width = out_ref.shape[0], out_ref.shape[3]

    def widen(i, carry):
        at = pl.ds(pl.multiple_of(i * 128, 128), 128)
        for k in range(quad * freqs // LANES):
            wide_ref[k, at, :] = block_ref[at, k * LANES : (k + 1) * LANES].astype(jnp.float32)
        return carry

    lax.fori_loop(0, 2 * length // 128, widen, 0)

    def row(r, carry):
        for col in range(quad):
            for c in range(2):
                m = (col % 2) * length + ((col // 2) * 2 + c) * groups
                for k in range(freqs // LANES):
                    part = wide_ref[col * (freqs // LANES) + k, pl.ds(r * 2 + c, groups, stride=2 * quad), :]
                    rhs_ref[m : m + groups, k * LANES : (k + 1) * LANES] = part.astype(jnp.bfloat16)
        even, odd = [
            dot(table_ref[3, parity], rhs_ref[parity * length : (parity + 1) * length, :]) for parity in range(2)
        ]
        for upper, total in ((0, even + odd), (1, even - odd)):
            total = total.astype(jnp.bfloat16)
            for c in range(2):
                part = total[c * (length // 2) : (c + 1) * (length // 2)]
                out_ref[upper * (targets // 2) : (upper + 1) * (targets // 2), c, r] = part.reshape(
                    targets // 2, width, freqs
                )
        return carry

    lax.fori_loop(0, quad, row, 0)


def in_vmem():
    return pl.BlockSpec(memory_space=pltpu.VMEM)


def call(kernel, out_shape, in_specs, scratch, flops, limit, name):
    return pl.pallas_call(
        kernel,
        out_shape=jax.ShapeDtypeStruct(out_shape, jnp.bfloat16),
        in_specs=in_specs,
        out_specs=in_vmem(),
        scratch_shapes=scratch,
        compiler_params=pltpu.CompilerParams(vmem_limit_bytes=limit * 2**20),
        cost_estimate=pl.CostEstimate(flops=flops, bytes_accessed=2**22, transcendentals=0),
        name=name,
    )


def per_device(green, vertex):
    kx, ky = lax.axis_size("kx"), lax.axis_size("ky")
    groups = kx * ky
    rows, width, freqs = green.shape[1:]
    length = width * ky
    quad = length // groups
    bosons = vertex.shape[1]
    n = 2 * length
    dfts = jnp.asarray(tables(length, groups))
    both = ("kx", "ky")

    block = green.reshape(2, ky, quad, width, freqs).transpose(1, 0, 2, 3, 4)
    block = lax.all_to_all(block, "ky", split_axis=0, concat_axis=0, tiled=True)
    spectrum = call(
        lambda *refs: columns_kernel(quad, groups, freqs, *refs),
        (n, quad * freqs),
        [in_vmem()] * 2,
        [pltpu.VMEM((quad * freqs // LANES, n, LANES), jnp.float32)],
        n * n * quad * freqs,
        16,
        "to_columns",
    )(block, dfts)
    spectrum = lax.all_to_all(spectrum, both, split_axis=0, concat_axis=0, tiled=True)
    field = call(
        lambda *refs: sites_kernel(quad, freqs, bosons, *refs),
        (n, quad * freqs),
        [in_vmem()] * 3,
        [pltpu.VMEM((quad, 4, length // 2, freqs), jnp.bfloat16)] * 2
        + [pltpu.VMEM((2, bosons, freqs, freqs), jnp.bfloat16)],
        2 * n * n * quad * freqs + 6 * bosons * length * quad * freqs * freqs,
        24,
        "on_sites",
    )(spectrum, dfts, vertex)
    field = lax.all_to_all(field, both, split_axis=0, concat_axis=0, tiled=True)
    settled = call(
        lambda *refs: rows_kernel(quad, groups, freqs, *refs),
        (ky, 2, quad, width, freqs),
        [in_vmem()] * 2,
        [pltpu.VMEM((quad * freqs // LANES, n, LANES), jnp.float32), pltpu.VMEM((n, freqs), jnp.bfloat16)],
        n * n * quad * freqs,
        16,
        "to_rows",
    )(field, dfts)
    settled = lax.all_to_all(settled, "ky", split_axis=0, concat_axis=0, tiled=True)
    return settled.transpose(1, 0, 2, 3, 4).reshape(2, rows, width, freqs).astype(jnp.float32)


def solution(mesh):
    placed = (P(None, "kx", "ky", None), P())
    return jax.shard_map(
        per_device, mesh=mesh, in_specs=placed, out_specs=P(None, "kx", "ky", None), check_vma=False
    )
```

```python
import math

import jax
import jax.numpy as jnp
import ml_dtypes
import numpy as np
from jax import lax
from jax.experimental import pallas as pl
from jax.experimental.pallas import tpu as pltpu
from jax.sharding import PartitionSpec as P

LANES = 128
TILE = 16
GROUP = 4


def pair_list(length):
    half = length // 2
    upper = (length - np.arange(half)) % length
    upper[0] = half
    return np.concatenate([np.arange(half), upper])


def complex_table(sites, momenta, length, direction, scale):
    phase = (sites[:, None].astype(np.int64) * momenta[None, :] % length) * (
        direction * 2.0 * math.pi / length
    )
    cos, sin = np.cos(phase) * scale, np.sin(phase) * scale
    return np.stack([np.stack([cos, -sin], 1), np.stack([sin, cos], 1)], 0)


def tables(length, groups, kx):
    quad = length // groups
    half = length // 2
    pairs = pair_list(length)
    low = np.arange(half)
    sent = low.reshape(kx // 2, groups // kx, quad).transpose(1, 0, 2).reshape(-1)
    own = np.stack([pairs[:half].reshape(groups, -1), pairs[half:].reshape(groups, -1)], 1).reshape(groups, quad)
    found = []
    for parity in range(2):
        y = own[:, parity::2].T.reshape(-1)
        x = np.concatenate([pairs[:half][parity::2], pairs[half:][parity::2]])
        cols = quad // 2
        t_y = complex_table(y, low, length, 1.0, 1.0)
        t_y = t_y.reshape(2, cols, groups, 2, half).transpose(1, 0, 2, 3, 4)
        t_x = complex_table(x, sent, length, 1.0, 1.0 / length).transpose(0, 1, 3, 2)
        b_x = complex_table(sent, x, length, -1.0, 1.0).transpose(1, 0, 2, 3)
        b_y = complex_table(low, y, length, -1.0, 1.0 / length)
        b_y = b_y.reshape(2, half, 2, cols, groups).transpose(0, 1, 3, 2, 4)
        found.append([t.reshape(length, length) for t in (t_y, t_x, b_x, b_y)])
    return np.stack([np.stack(f) for f in found], 1).astype(ml_dtypes.bfloat16)


def dot(left, right):
    return jnp.dot(left, right, preferred_element_type=jnp.float32)


def dot_turned(left, right):
    return lax.dot_general(left, right, (((1,), (1,)), ((), ())), preferred_element_type=jnp.float32)


def columns_kernel(quad, groups, freqs, block_ref, table_ref, out_ref, wide_ref):
    length = quad * groups

    def row(r, carry):
        both = [block_ref[:, c, r].reshape(length, freqs) for c in range(2)]
        low, high = [b[: length // 2] for b in both], [b[length // 2 :] for b in both]
        for parity in range(2):
            rhs = jnp.concatenate([a - b if parity else a + b for a, b in zip(low, high)], 0)
            product = dot(table_ref[0, parity], rhs)
            for at in range(quad):
                col, c = 2 * (at // 2) + parity, at % 2
                part = product[at * groups : (at + 1) * groups]
                for k in range(freqs // LANES):
                    spots = pl.ds(r * 2 + c, groups, stride=2 * quad)
                    wide_ref[col * (freqs // LANES) + k, spots, :] = part[:, k * LANES : (k + 1) * LANES]
        return carry

    lax.fori_loop(0, quad, row, 0)

    def settle(i, carry):
        at = pl.ds(pl.multiple_of(i * 128, 128), 128)
        for k in range(quad * freqs // LANES):
            out_ref[at, k * LANES : (k + 1) * LANES] = wide_ref[k, at, :].astype(jnp.bfloat16)
        return carry

    lax.fori_loop(0, 2 * length // 128, settle, 0)


def shifted(values, by):
    if by == 0:
        return values
    tail = jnp.zeros((values.shape[0], by), values.dtype)
    return jnp.concatenate([values[:, by:], tail], 1)


def swap_first(ref, col, c):
    low, high = ref[col, 2 * c, :TILE, :], ref[col, 2 * c + 1, :TILE, :]
    top = lax.broadcasted_iota(jnp.int32, low.shape, 0) == 0
    ref[col, 2 * c, :TILE, :] = jnp.where(top, high, low)
    ref[col, 2 * c + 1, :TILE, :] = jnp.where(top, low, high)


def sites_kernel(quad, kx, freqs, bosons, block_ref, table_ref, vertex_ref, out_ref, green_ref, field_ref, mixed_ref):
    half = green_ref.shape[2]
    length = 2 * half
    part = half // 2
    first = lax.axis_index("kx") + lax.axis_index("ky") == 0

    run = kx * quad
    sent = block_ref[...].reshape(length // run, 2, run, quad * freqs)
    low, high = [sent[:, i].reshape(length, quad * freqs) for i in range(2)]
    for parity in range(2):
        lattice = dot(table_ref[1, parity], low - high if parity else low + high).astype(jnp.bfloat16)
        for at in range(4):
            for col in range(quad):
                green_ref[col, at, parity * part : (parity + 1) * part, :] = lattice[
                    at * part : (at + 1) * part, col * freqs : (col + 1) * freqs
                ]
    for col in range(quad // 2, quad):
        for c in range(2):
            swap_first(green_ref, col, c)
    for w in range(bosons):
        v_re, v_im = vertex_ref[0, w], vertex_ref[1, w]
        mixed_ref[0, w] = v_im - v_re
        mixed_ref[1, w] = v_re + v_im

    def pair_block(step, carry):
        column, side = step // 2, step % 2
        alone = jnp.logical_and(first, column == 0)
        p_col = jnp.where(alone, side * (quad // 2), column)
        q_col = jnp.where(alone, side * (quad // 2), column + quad // 2)
        p_re, p_im = green_ref[p_col, side], green_ref[p_col, 2 + side]
        q_re, q_im = green_ref[q_col, 1 - side], green_ref[q_col, 3 - side]
        row = lax.broadcasted_iota(jnp.int32, (TILE, freqs), 0)
        own = jnp.logical_and(row == 0, alone)

        def mirror(mine, other):
            return jnp.concatenate([jnp.where(own, mine[:TILE], other[:TILE]), other[TILE:]], 0)

        totals = [jnp.zeros((half, freqs), jnp.float32) for _ in range(4)]
        for start in range(0, bosons, GROUP):
            sums = None
            for w in range(start, min(start + GROUP, bosons)):
                sp_re, sp_im = shifted(p_re, w), shifted(p_im, w)
                sq_re, sq_im = shifted(q_re, w), shifted(q_im, w)
                b_re, b_im = [], []
                for g_re, g_im, m_re, m_im in (
                    (p_re, p_im, mirror(sp_re, sq_re), mirror(sp_im, sq_im)),
                    (q_re, q_im, mirror(sq_re, sp_re), mirror(sq_im, sp_im)),
                ):
                    b_re.append(g_re * m_re - g_im * m_im)
                    b_im.append(g_re * m_im + g_im * m_re)
                b_re, b_im = jnp.concatenate(b_re, 0), jnp.concatenate(b_im, 0)
                shared = dot_turned(b_re + b_im, vertex_ref[0, w])
                c_re = (shared - dot_turned(b_im, mixed_ref[1, w])).astype(jnp.bfloat16)
                c_im = (shared + dot_turned(b_re, mixed_ref[0, w])).astype(jnp.bfloat16)
                cp_re, cq_re, cp_im, cq_im = c_re[:half], c_re[half:], c_im[:half], c_im[half:]
                terms = [
                    sp_re * cp_re - sp_im * cp_im,
                    sp_re * cp_im + sp_im * cp_re,
                    sq_re * cq_re - sq_im * cq_im,
                    sq_re * cq_im + sq_im * cq_re,
                ]
                sums = terms if sums is None else [s + t for s, t in zip(sums, terms)]
            totals = [t + s.astype(jnp.float32) for t, s in zip(totals, sums)]
        p_sum_re, p_sum_im, q_sum_re, q_sum_im = [t.astype(jnp.bfloat16) for t in totals]
        field_ref[p_col, side] = p_sum_re
        field_ref[p_col, 2 + side] = p_sum_im
        field_ref[q_col, 1 - side] = q_sum_re
        field_ref[q_col, 3 - side] = q_sum_im
        return carry

    lax.fori_loop(0, quad, pair_block, 0)

    for col in range(quad // 2, quad):
        for c in range(2):
            swap_first(field_ref, col, c)
    for col in range(quad):
        lanes = slice(col * freqs, (col + 1) * freqs)
        even, odd = [
            dot(
                table_ref[2, parity],
                field_ref[col, :, parity * part : (parity + 1) * part, :].reshape(length, freqs),
            )
            for parity in range(2)
        ]
        for upper, total in ((0, even + odd), (1, even - odd)):
            total = total.astype(jnp.bfloat16)
            for k in range(length // run):
                at = (2 * k + upper) * run
                out_ref[at : at + run, lanes] = total[k * run : (k + 1) * run]


def rows_kernel(quad, groups, freqs, block_ref, table_ref, out_ref, wide_ref, rhs_ref):
    length = quad * groups
    targets, width = out_ref.shape[0], out_ref.shape[3]

    def widen(i, carry):
        at = pl.ds(pl.multiple_of(i * 128, 128), 128)
        for k in range(quad * freqs // LANES):
            wide_ref[k, at, :] = block_ref[at, k * LANES : (k + 1) * LANES].astype(jnp.float32)
        return carry

    lax.fori_loop(0, 2 * length // 128, widen, 0)

    def row(r, carry):
        for col in range(quad):
            for c in range(2):
                m = (col % 2) * length + ((col // 2) * 2 + c) * groups
                for k in range(freqs // LANES):
                    part = wide_ref[col * (freqs // LANES) + k, pl.ds(r * 2 + c, groups, stride=2 * quad), :]
                    rhs_ref[m : m + groups, k * LANES : (k + 1) * LANES] = part.astype(jnp.bfloat16)
        even, odd = [
            dot(table_ref[3, parity], rhs_ref[parity * length : (parity + 1) * length, :]) for parity in range(2)
        ]
        for upper, total in ((0, even + odd), (1, even - odd)):
            total = total.astype(jnp.bfloat16)
            for c in range(2):
                part = total[c * (length // 2) : (c + 1) * (length // 2)]
                out_ref[upper * (targets // 2) : (upper + 1) * (targets // 2), c, r] = part.reshape(
                    targets // 2, width, freqs
                )
        return carry

    lax.fori_loop(0, quad, row, 0)


def settle_kernel(devices, quad, block_ref, out_hbm, wide_ref, sems):
    copies = []
    for c in range(2):
        for d in range(devices):
            wide_ref[c, d] = block_ref[d, c].astype(jnp.float32)
            copy = pltpu.make_async_copy(wide_ref.at[c, d], out_hbm.at[c, pl.ds(d * quad, quad)], sems.at[c, d])
            copy.start()
            copies.append(copy)
    for copy in copies:
        copy.wait()


def in_vmem():
    return pl.BlockSpec(memory_space=pltpu.VMEM)


def call(kernel, out_shape, in_specs, scratch, flops, limit, name):
    return pl.pallas_call(
        kernel,
        out_shape=jax.ShapeDtypeStruct(out_shape, jnp.bfloat16),
        in_specs=in_specs,
        out_specs=in_vmem(),
        scratch_shapes=scratch,
        compiler_params=pltpu.CompilerParams(vmem_limit_bytes=limit * 2**20),
        cost_estimate=pl.CostEstimate(flops=flops, bytes_accessed=2**22, transcendentals=0),
        name=name,
    )


def per_device(green, vertex):
    kx, ky = lax.axis_size("kx"), lax.axis_size("ky")
    groups = kx * ky
    rows, width, freqs = green.shape[1:]
    length = width * ky
    quad = length // groups
    bosons = vertex.shape[1]
    n = 2 * length
    dfts = jnp.asarray(tables(length, groups, kx))
    both = ("ky", "kx")

    block = green.reshape(2, ky, quad, width, freqs).transpose(1, 0, 2, 3, 4)
    block = lax.all_to_all(block, "ky", split_axis=0, concat_axis=0, tiled=True)
    spectrum = call(
        lambda *refs: columns_kernel(quad, groups, freqs, *refs),
        (n, quad * freqs),
        [in_vmem()] * 2,
        [pltpu.VMEM((quad * freqs // LANES, n, LANES), jnp.float32)],
        n * n * quad * freqs,
        16,
        "to_columns",
    )(block, dfts)
    spectrum = lax.all_to_all(spectrum, both, split_axis=0, concat_axis=0, tiled=True)
    field = call(
        lambda *refs: sites_kernel(quad, kx, freqs, bosons, *refs),
        (n, quad * freqs),
        [in_vmem()] * 3,
        [pltpu.VMEM((quad, 4, length // 2, freqs), jnp.bfloat16)] * 2
        + [pltpu.VMEM((2, bosons, freqs, freqs), jnp.bfloat16)],
        2 * n * n * quad * freqs + 6 * bosons * length * quad * freqs * freqs,
        24,
        "on_sites",
    )(spectrum, dfts, vertex)
    field = lax.all_to_all(field, both, split_axis=0, concat_axis=0, tiled=True)
    settled = call(
        lambda *refs: rows_kernel(quad, groups, freqs, *refs),
        (ky, 2, quad, width, freqs),
        [in_vmem()] * 2,
        [pltpu.VMEM((quad * freqs // LANES, n, LANES), jnp.float32), pltpu.VMEM((n, freqs), jnp.bfloat16)],
        n * n * quad * freqs,
        16,
        "to_rows",
    )(field, dfts)
    settled = lax.all_to_all(settled, "ky", split_axis=0, concat_axis=0, tiled=True)
    return pl.pallas_call(
        lambda *refs: settle_kernel(ky, quad, *refs),
        out_shape=jax.ShapeDtypeStruct((2, rows, width, freqs), jnp.float32),
        in_specs=[in_vmem()],
        out_specs=pl.BlockSpec(memory_space=pltpu.HBM),
        scratch_shapes=[
            pltpu.VMEM((2, ky, quad, width, freqs), jnp.float32),
            pltpu.SemaphoreType.DMA((2, ky)),
        ],
        compiler_params=pltpu.CompilerParams(vmem_limit_bytes=12 * 2**20),
        name="to_output",
    )(settled)


def solution(mesh):
    placed = (P(None, "kx", "ky", None), P())
    return jax.shard_map(
        per_device, mesh=mesh, in_specs=placed, out_specs=P(None, "kx", "ky", None), check_vma=False
    )
```

```python
import math

import jax
import jax.numpy as jnp
import ml_dtypes
import numpy as np
from jax import lax
from jax.experimental import pallas as pl
from jax.experimental.pallas import tpu as pltpu
from jax.sharding import PartitionSpec as P

LANES = 128
TILE = 16
GROUP = 4


def pair_list(length):
    half = length // 2
    upper = (length - np.arange(half)) % length
    upper[0] = half
    return np.concatenate([np.arange(half), upper])


def complex_table(sites, momenta, length, direction, scale):
    phase = (sites[:, None].astype(np.int64) * momenta[None, :] % length) * (
        direction * 2.0 * math.pi / length
    )
    cos, sin = np.cos(phase) * scale, np.sin(phase) * scale
    return np.stack([np.stack([cos, -sin], 1), np.stack([sin, cos], 1)], 0)


def tables(length, groups, kx):
    quad = length // groups
    half = length // 2
    pairs = pair_list(length)
    low = np.arange(half)
    sent = low.reshape(kx // 2, groups // kx, quad).transpose(1, 0, 2).reshape(-1)
    own = np.stack([pairs[:half].reshape(groups, -1), pairs[half:].reshape(groups, -1)], 1).reshape(groups, quad)
    found = []
    for parity in range(2):
        y = own[:, parity::2].T.reshape(-1)
        x = np.concatenate([pairs[:half][parity::2], pairs[half:][parity::2]])
        cols = quad // 2
        t_y = complex_table(y, low, length, 1.0, 1.0)
        t_y = t_y.reshape(2, cols, groups, 2, half).transpose(1, 0, 2, 3, 4)
        t_x = complex_table(x, sent, length, 1.0, 1.0 / length).transpose(0, 1, 3, 2)
        b_x = complex_table(sent, x, length, -1.0, 1.0).transpose(1, 0, 2, 3)
        b_y = complex_table(low, y, length, -1.0, 1.0 / length)
        b_y = b_y.reshape(2, half, 2, cols, groups).transpose(0, 1, 3, 2, 4)
        found.append([t.reshape(length, length) for t in (t_y, t_x, b_x, b_y)])
    return np.stack([np.stack(f) for f in found], 1).astype(ml_dtypes.bfloat16)


def dot(left, right):
    return jnp.dot(left, right, preferred_element_type=jnp.float32)


def dot_turned(left, right):
    return lax.dot_general(left, right, (((1,), (1,)), ((), ())), preferred_element_type=jnp.float32)


def columns_kernel(quad, groups, freqs, block_ref, table_ref, out_ref, wide_ref):
    length = quad * groups

    def row(r, carry):
        both = [block_ref[:, c, r].reshape(length, freqs) for c in range(2)]
        low, high = [b[: length // 2] for b in both], [b[length // 2 :] for b in both]
        for parity in range(2):
            rhs = jnp.concatenate([a - b if parity else a + b for a, b in zip(low, high)], 0)
            product = dot(table_ref[0, parity], rhs)
            for at in range(quad):
                col, c = 2 * (at // 2) + parity, at % 2
                part = product[at * groups : (at + 1) * groups]
                for k in range(freqs // LANES):
                    spots = pl.ds(r * 2 + c, groups, stride=2 * quad)
                    wide_ref[col * (freqs // LANES) + k, spots, :] = part[:, k * LANES : (k + 1) * LANES]
        return carry

    for r in range(quad):
        row(r, 0)

    def settle(i, carry):
        at = pl.ds(pl.multiple_of(i * 128, 128), 128)
        for k in range(quad * freqs // LANES):
            out_ref[at, k * LANES : (k + 1) * LANES] = wide_ref[k, at, :].astype(jnp.bfloat16)
        return carry

    lax.fori_loop(0, 2 * length // 128, settle, 0)


def shifted(values, by):
    if by == 0:
        return values
    tail = jnp.zeros((values.shape[0], by), values.dtype)
    return jnp.concatenate([values[:, by:], tail], 1)


def swap_first(ref, col, c):
    low, high = ref[col, 2 * c, :TILE, :], ref[col, 2 * c + 1, :TILE, :]
    top = lax.broadcasted_iota(jnp.int32, low.shape, 0) == 0
    ref[col, 2 * c, :TILE, :] = jnp.where(top, high, low)
    ref[col, 2 * c + 1, :TILE, :] = jnp.where(top, low, high)


def sites_kernel(quad, kx, freqs, bosons, block_ref, table_ref, vertex_ref, out_ref, green_ref, field_ref, mixed_ref):
    half = green_ref.shape[2]
    length = 2 * half
    part = half // 2
    first = lax.axis_index("kx") + lax.axis_index("ky") == 0

    run = kx * quad
    sent = block_ref[...].reshape(length // run, 2, run, quad * freqs)
    low, high = [sent[:, i].reshape(length, quad * freqs) for i in range(2)]
    for parity in range(2):
        lattice = dot(table_ref[1, parity], low - high if parity else low + high).astype(jnp.bfloat16)
        for at in range(4):
            for col in range(quad):
                green_ref[col, at, parity * part : (parity + 1) * part, :] = lattice[
                    at * part : (at + 1) * part, col * freqs : (col + 1) * freqs
                ]
    for col in range(quad // 2, quad):
        for c in range(2):
            swap_first(green_ref, col, c)
    for w in range(bosons):
        v_re, v_im = vertex_ref[0, w], vertex_ref[1, w]
        mixed_ref[0, w] = v_im - v_re
        mixed_ref[1, w] = v_re + v_im

    def pair_block(step, carry):
        column, side = step // 2, step % 2
        alone = jnp.logical_and(first, column == 0)
        p_col = jnp.where(alone, side * (quad // 2), column)
        q_col = jnp.where(alone, side * (quad // 2), column + quad // 2)
        p_re, p_im = green_ref[p_col, side], green_ref[p_col, 2 + side]
        q_re, q_im = green_ref[q_col, 1 - side], green_ref[q_col, 3 - side]
        row = lax.broadcasted_iota(jnp.int32, (TILE, freqs), 0)
        own = jnp.logical_and(row == 0, alone)

        def mirror(mine, other):
            return jnp.concatenate([jnp.where(own, mine[:TILE], other[:TILE]), other[TILE:]], 0)

        totals = [jnp.zeros((half, freqs), jnp.float32) for _ in range(4)]
        for start in range(0, bosons, GROUP):
            sums = None
            for w in range(start, min(start + GROUP, bosons)):
                sp_re, sp_im = shifted(p_re, w), shifted(p_im, w)
                sq_re, sq_im = shifted(q_re, w), shifted(q_im, w)
                b_re, b_im = [], []
                for g_re, g_im, m_re, m_im in (
                    (p_re, p_im, mirror(sp_re, sq_re), mirror(sp_im, sq_im)),
                    (q_re, q_im, mirror(sq_re, sp_re), mirror(sq_im, sp_im)),
                ):
                    b_re.append(g_re * m_re - g_im * m_im)
                    b_im.append(g_re * m_im + g_im * m_re)
                b_re, b_im = jnp.concatenate(b_re, 0), jnp.concatenate(b_im, 0)
                shared = dot_turned(b_re + b_im, vertex_ref[0, w])
                c_re = (shared - dot_turned(b_im, mixed_ref[1, w])).astype(jnp.bfloat16)
                c_im = (shared + dot_turned(b_re, mixed_ref[0, w])).astype(jnp.bfloat16)
                cp_re, cq_re, cp_im, cq_im = c_re[:half], c_re[half:], c_im[:half], c_im[half:]
                terms = [
                    sp_re * cp_re - sp_im * cp_im,
                    sp_re * cp_im + sp_im * cp_re,
                    sq_re * cq_re - sq_im * cq_im,
                    sq_re * cq_im + sq_im * cq_re,
                ]
                sums = terms if sums is None else [s + t for s, t in zip(sums, terms)]
            totals = [t + s.astype(jnp.float32) for t, s in zip(totals, sums)]
        p_sum_re, p_sum_im, q_sum_re, q_sum_im = [t.astype(jnp.bfloat16) for t in totals]
        field_ref[p_col, side] = p_sum_re
        field_ref[p_col, 2 + side] = p_sum_im
        field_ref[q_col, 1 - side] = q_sum_re
        field_ref[q_col, 3 - side] = q_sum_im
        return carry

    lax.fori_loop(0, quad, pair_block, 0)

    for col in range(quad // 2, quad):
        for c in range(2):
            swap_first(field_ref, col, c)
    for col in range(quad):
        lanes = slice(col * freqs, (col + 1) * freqs)
        even, odd = [
            dot(
                table_ref[2, parity],
                field_ref[col, :, parity * part : (parity + 1) * part, :].reshape(length, freqs),
            )
            for parity in range(2)
        ]
        for upper, total in ((0, even + odd), (1, even - odd)):
            total = total.astype(jnp.bfloat16)
            for k in range(length // run):
                at = (2 * k + upper) * run
                out_ref[at : at + run, lanes] = total[k * run : (k + 1) * run]


def rows_kernel(quad, groups, freqs, block_ref, table_ref, out_ref, wide_ref, rhs_ref):
    length = quad * groups
    targets, width = out_ref.shape[0], out_ref.shape[3]

    def widen(i, carry):
        at = pl.ds(pl.multiple_of(i * 128, 128), 128)
        for k in range(quad * freqs // LANES):
            wide_ref[k, at, :] = block_ref[at, k * LANES : (k + 1) * LANES].astype(jnp.float32)
        return carry

    lax.fori_loop(0, 2 * length // 128, widen, 0)

    def row(r, carry):
        for col in range(quad):
            for c in range(2):
                m = (col % 2) * length + ((col // 2) * 2 + c) * groups
                for k in range(freqs // LANES):
                    part = wide_ref[col * (freqs // LANES) + k, pl.ds(r * 2 + c, groups, stride=2 * quad), :]
                    rhs_ref[r, m : m + groups, k * LANES : (k + 1) * LANES] = part.astype(jnp.bfloat16)
        even, odd = [
            dot(table_ref[3, parity], rhs_ref[r, parity * length : (parity + 1) * length, :]) for parity in range(2)
        ]
        for upper, total in ((0, even + odd), (1, even - odd)):
            total = total.astype(jnp.bfloat16)
            for c in range(2):
                part = total[c * (length // 2) : (c + 1) * (length // 2)]
                out_ref[upper * (targets // 2) : (upper + 1) * (targets // 2), c, r] = part.reshape(
                    targets // 2, width, freqs
                )
        return carry

    for r in range(quad):
        row(r, 0)


def settle_kernel(devices, quad, block_ref, out_hbm, wide_ref, sems):
    copies = []
    for c in range(2):
        for d in range(devices):
            wide_ref[c, d] = block_ref[d, c].astype(jnp.float32)
            copy = pltpu.make_async_copy(wide_ref.at[c, d], out_hbm.at[c, pl.ds(d * quad, quad)], sems.at[c, d])
            copy.start()
            copies.append(copy)
    for copy in copies:
        copy.wait()


def in_vmem():
    return pl.BlockSpec(memory_space=pltpu.VMEM)


def call(kernel, out_shape, in_specs, scratch, flops, limit, name):
    return pl.pallas_call(
        kernel,
        out_shape=jax.ShapeDtypeStruct(out_shape, jnp.bfloat16),
        in_specs=in_specs,
        out_specs=in_vmem(),
        scratch_shapes=scratch,
        compiler_params=pltpu.CompilerParams(vmem_limit_bytes=limit * 2**20),
        cost_estimate=pl.CostEstimate(flops=flops, bytes_accessed=2**22, transcendentals=0),
        name=name,
    )


def per_device(green, vertex):
    kx, ky = lax.axis_size("kx"), lax.axis_size("ky")
    groups = kx * ky
    rows, width, freqs = green.shape[1:]
    length = width * ky
    quad = length // groups
    bosons = vertex.shape[1]
    n = 2 * length
    dfts = jnp.asarray(tables(length, groups, kx))
    both = ("ky", "kx")

    block = green.reshape(2, ky, quad, width, freqs).transpose(1, 0, 2, 3, 4)
    block = lax.all_to_all(block, "ky", split_axis=0, concat_axis=0, tiled=True)
    spectrum = call(
        lambda *refs: columns_kernel(quad, groups, freqs, *refs),
        (n, quad * freqs),
        [in_vmem()] * 2,
        [pltpu.VMEM((quad * freqs // LANES, n, LANES), jnp.float32)],
        n * n * quad * freqs,
        16,
        "to_columns",
    )(block, dfts)
    spectrum = lax.all_to_all(spectrum, both, split_axis=0, concat_axis=0, tiled=True)
    field = call(
        lambda *refs: sites_kernel(quad, kx, freqs, bosons, *refs),
        (n, quad * freqs),
        [in_vmem()] * 3,
        [pltpu.VMEM((quad, 4, length // 2, freqs), jnp.bfloat16)] * 2
        + [pltpu.VMEM((2, bosons, freqs, freqs), jnp.bfloat16)],
        2 * n * n * quad * freqs + 6 * bosons * length * quad * freqs * freqs,
        24,
        "on_sites",
    )(spectrum, dfts, vertex)
    field = lax.all_to_all(field, both, split_axis=0, concat_axis=0, tiled=True)
    settled = call(
        lambda *refs: rows_kernel(quad, groups, freqs, *refs),
        (ky, 2, quad, width, freqs),
        [in_vmem()] * 2,
        [pltpu.VMEM((quad * freqs // LANES, n, LANES), jnp.float32), pltpu.VMEM((quad, n, freqs), jnp.bfloat16)],
        n * n * quad * freqs,
        16,
        "to_rows",
    )(field, dfts)
    settled = lax.all_to_all(settled, "ky", split_axis=0, concat_axis=0, tiled=True)
    return pl.pallas_call(
        lambda *refs: settle_kernel(ky, quad, *refs),
        out_shape=jax.ShapeDtypeStruct((2, rows, width, freqs), jnp.float32),
        in_specs=[in_vmem()],
        out_specs=pl.BlockSpec(memory_space=pltpu.HBM),
        scratch_shapes=[
            pltpu.VMEM((2, ky, quad, width, freqs), jnp.float32),
            pltpu.SemaphoreType.DMA((2, ky)),
        ],
        compiler_params=pltpu.CompilerParams(vmem_limit_bytes=12 * 2**20),
        name="to_output",
    )(settled)


def solution(mesh):
    placed = (P(None, "kx", "ky", None), P())
    return jax.shard_map(
        per_device, mesh=mesh, in_specs=placed, out_specs=P(None, "kx", "ky", None), check_vma=False
    )
```

```python
import math

import jax
import jax.numpy as jnp
import ml_dtypes
import numpy as np
from jax import lax
from jax.experimental import pallas as pl
from jax.experimental.pallas import tpu as pltpu
from jax.sharding import PartitionSpec as P

LANES = 128
TILE = 16
GROUP = 6


def pair_list(length):
    half = length // 2
    upper = (length - np.arange(half)) % length
    upper[0] = half
    return np.concatenate([np.arange(half), upper])


def complex_table(sites, momenta, length, direction, scale):
    phase = (sites[:, None].astype(np.int64) * momenta[None, :] % length) * (
        direction * 2.0 * math.pi / length
    )
    cos, sin = np.cos(phase) * scale, np.sin(phase) * scale
    return np.stack([np.stack([cos, -sin], 1), np.stack([sin, cos], 1)], 0)


def tables(length, groups, kx):
    quad = length // groups
    half = length // 2
    pairs = pair_list(length)
    low = np.arange(half)
    sent = low.reshape(kx // 2, groups // kx, quad).transpose(1, 0, 2).reshape(-1)
    own = np.stack([pairs[:half].reshape(groups, -1), pairs[half:].reshape(groups, -1)], 1).reshape(groups, quad)
    found = []
    for parity in range(2):
        y = own[:, parity::2].T.reshape(-1)
        x = np.concatenate([pairs[:half][parity::2], pairs[half:][parity::2]])
        cols = quad // 2
        t_y = complex_table(y, low, length, 1.0, 1.0)
        t_y = t_y.reshape(2, cols, groups, 2, half).transpose(1, 0, 2, 3, 4)
        t_x = complex_table(x, sent, length, 1.0, 1.0 / length).transpose(0, 1, 3, 2)
        b_x = complex_table(sent, x, length, -1.0, 1.0).transpose(1, 0, 2, 3)
        b_y = complex_table(low, y, length, -1.0, 1.0 / length)
        b_y = b_y.reshape(2, half, 2, cols, groups).transpose(0, 1, 3, 2, 4)
        found.append([t.reshape(length, length) for t in (t_y, t_x, b_x, b_y)])
    return np.stack([np.stack(f) for f in found], 1).astype(ml_dtypes.bfloat16)


def dot(left, right):
    return jnp.dot(left, right, preferred_element_type=jnp.float32)


def dot_turned(left, right):
    return lax.dot_general(left, right, (((1,), (1,)), ((), ())), preferred_element_type=jnp.float32)


def columns_kernel(quad, groups, freqs, block_ref, table_ref, out_ref, wide_ref):
    length = quad * groups

    def row(r, carry):
        both = [block_ref[:, c, r].reshape(length, freqs) for c in range(2)]
        low, high = [b[: length // 2] for b in both], [b[length // 2 :] for b in both]
        for parity in range(2):
            rhs = jnp.concatenate([a - b if parity else a + b for a, b in zip(low, high)], 0)
            product = dot(table_ref[0, parity], rhs)
            for at in range(quad):
                col, c = 2 * (at // 2) + parity, at % 2
                part = product[at * groups : (at + 1) * groups]
                for k in range(freqs // LANES):
                    spots = pl.ds(r * 2 + c, groups, stride=2 * quad)
                    wide_ref[col * (freqs // LANES) + k, spots, :] = part[:, k * LANES : (k + 1) * LANES]
        return carry

    for r in range(quad):
        row(r, 0)

    def settle(i, carry):
        at = pl.ds(pl.multiple_of(i * 128, 128), 128)
        for k in range(quad * freqs // LANES):
            out_ref[at, k * LANES : (k + 1) * LANES] = wide_ref[k, at, :].astype(jnp.bfloat16)
        return carry

    lax.fori_loop(0, 2 * length // 128, settle, 0, unroll=True)


def shifted(values, by):
    if by == 0:
        return values
    tail = jnp.zeros((values.shape[0], by), values.dtype)
    return jnp.concatenate([values[:, by:], tail], 1)


def swap_first(ref, col, c):
    low, high = ref[col, 2 * c, :TILE, :], ref[col, 2 * c + 1, :TILE, :]
    top = lax.broadcasted_iota(jnp.int32, low.shape, 0) == 0
    ref[col, 2 * c, :TILE, :] = jnp.where(top, high, low)
    ref[col, 2 * c + 1, :TILE, :] = jnp.where(top, low, high)


def sites_kernel(quad, kx, freqs, bosons, block_ref, table_ref, vertex_ref, out_ref, green_ref, field_ref, mixed_ref):
    half = green_ref.shape[2]
    length = 2 * half
    part = half // 2
    first = lax.axis_index("kx") + lax.axis_index("ky") == 0

    run = kx * quad
    sent = block_ref[...].reshape(length // run, 2, run, quad * freqs)
    low, high = [sent[:, i].reshape(length, quad * freqs) for i in range(2)]
    for parity in range(2):
        lattice = dot(table_ref[1, parity], low - high if parity else low + high).astype(jnp.bfloat16)
        for at in range(4):
            for col in range(quad):
                green_ref[col, at, parity * part : (parity + 1) * part, :] = lattice[
                    at * part : (at + 1) * part, col * freqs : (col + 1) * freqs
                ]
    for col in range(quad // 2, quad):
        for c in range(2):
            swap_first(green_ref, col, c)
    for w in range(bosons):
        v_re, v_im = vertex_ref[0, w], vertex_ref[1, w]
        mixed_ref[0, w] = v_im - v_re
        mixed_ref[1, w] = v_re + v_im

    def pair_block(step, carry):
        column, side = step // 2, step % 2
        alone = jnp.logical_and(first, column == 0)
        p_col = jnp.where(alone, side * (quad // 2), column)
        q_col = jnp.where(alone, side * (quad // 2), column + quad // 2)
        p_re, p_im = green_ref[p_col, side], green_ref[p_col, 2 + side]
        q_re, q_im = green_ref[q_col, 1 - side], green_ref[q_col, 3 - side]
        row = lax.broadcasted_iota(jnp.int32, (TILE, freqs), 0)
        own = jnp.logical_and(row == 0, alone)

        def mirror(mine, other):
            return jnp.concatenate([jnp.where(own, mine[:TILE], other[:TILE]), other[TILE:]], 0)

        totals = [jnp.zeros((half, freqs), jnp.float32) for _ in range(4)]
        for start in range(0, bosons, GROUP):
            sums = None
            for w in range(start, min(start + GROUP, bosons)):
                sp_re, sp_im = shifted(p_re, w), shifted(p_im, w)
                sq_re, sq_im = shifted(q_re, w), shifted(q_im, w)
                b_re, b_im = [], []
                for g_re, g_im, m_re, m_im in (
                    (p_re, p_im, mirror(sp_re, sq_re), mirror(sp_im, sq_im)),
                    (q_re, q_im, mirror(sq_re, sp_re), mirror(sq_im, sp_im)),
                ):
                    b_re.append(g_re * m_re - g_im * m_im)
                    b_im.append(g_re * m_im + g_im * m_re)
                b_re, b_im = jnp.concatenate(b_re, 0), jnp.concatenate(b_im, 0)
                if w % 2:
                    panel = jnp.concatenate([vertex_ref[0, w], vertex_ref[1, w]], 1)
                    c_re = dot_turned(jnp.concatenate([b_re, -b_im], 1), panel).astype(jnp.bfloat16)
                    c_im = dot_turned(jnp.concatenate([b_im, b_re], 1), panel).astype(jnp.bfloat16)
                else:
                    shared = dot_turned(b_re + b_im, vertex_ref[0, w])
                    c_re = (shared - dot_turned(b_im, mixed_ref[1, w])).astype(jnp.bfloat16)
                    c_im = (shared + dot_turned(b_re, mixed_ref[0, w])).astype(jnp.bfloat16)
                cp_re, cq_re, cp_im, cq_im = c_re[:half], c_re[half:], c_im[:half], c_im[half:]
                terms = [
                    sp_re * cp_re - sp_im * cp_im,
                    sp_re * cp_im + sp_im * cp_re,
                    sq_re * cq_re - sq_im * cq_im,
                    sq_re * cq_im + sq_im * cq_re,
                ]
                sums = terms if sums is None else [s + t for s, t in zip(sums, terms)]
            totals = [t + s.astype(jnp.float32) for t, s in zip(totals, sums)]
        p_sum_re, p_sum_im, q_sum_re, q_sum_im = [t.astype(jnp.bfloat16) for t in totals]
        field_ref[p_col, side] = p_sum_re
        field_ref[p_col, 2 + side] = p_sum_im
        field_ref[q_col, 1 - side] = q_sum_re
        field_ref[q_col, 3 - side] = q_sum_im
        return carry

    lax.fori_loop(0, quad, pair_block, 0)

    for col in range(quad // 2, quad):
        for c in range(2):
            swap_first(field_ref, col, c)
    for col in range(quad):
        lanes = slice(col * freqs, (col + 1) * freqs)
        even, odd = [
            dot(
                table_ref[2, parity],
                field_ref[col, :, parity * part : (parity + 1) * part, :].reshape(length, freqs),
            )
            for parity in range(2)
        ]
        for upper, total in ((0, even + odd), (1, even - odd)):
            total = total.astype(jnp.bfloat16)
            for k in range(length // run):
                at = (2 * k + upper) * run
                out_ref[at : at + run, lanes] = total[k * run : (k + 1) * run]


def rows_kernel(quad, groups, freqs, block_ref, table_ref, out_ref, wide_ref, rhs_ref):
    length = quad * groups
    targets, width = out_ref.shape[0], out_ref.shape[3]

    def widen(i, carry):
        at = pl.ds(pl.multiple_of(i * 128, 128), 128)
        for k in range(quad * freqs // LANES):
            wide_ref[k, at, :] = block_ref[at, k * LANES : (k + 1) * LANES].astype(jnp.float32)
        return carry

    lax.fori_loop(0, 2 * length // 128, widen, 0, unroll=True)

    def row(r, carry):
        for col in range(quad):
            for c in range(2):
                m = (col % 2) * length + ((col // 2) * 2 + c) * groups
                for k in range(freqs // LANES):
                    part = wide_ref[col * (freqs // LANES) + k, pl.ds(r * 2 + c, groups, stride=2 * quad), :]
                    rhs_ref[r, m : m + groups, k * LANES : (k + 1) * LANES] = part.astype(jnp.bfloat16)
        even, odd = [
            dot(table_ref[3, parity], rhs_ref[r, parity * length : (parity + 1) * length, :]) for parity in range(2)
        ]
        for upper, total in ((0, even + odd), (1, even - odd)):
            total = total.astype(jnp.bfloat16)
            for c in range(2):
                part = total[c * (length // 2) : (c + 1) * (length // 2)]
                out_ref[upper * (targets // 2) : (upper + 1) * (targets // 2), c, r] = part.reshape(
                    targets // 2, width, freqs
                )
        return carry

    for r in range(quad):
        row(r, 0)


def settle_kernel(devices, quad, block_ref, out_hbm, wide_ref, sems):
    copies = []
    for c in range(2):
        for d in range(devices):
            wide_ref[c, d] = block_ref[d, c].astype(jnp.float32)
            copy = pltpu.make_async_copy(wide_ref.at[c, d], out_hbm.at[c, pl.ds(d * quad, quad)], sems.at[c, d])
            copy.start()
            copies.append(copy)
    for copy in copies:
        copy.wait()


def in_vmem():
    return pl.BlockSpec(memory_space=pltpu.VMEM)


def call(kernel, out_shape, in_specs, scratch, flops, limit, name):
    return pl.pallas_call(
        kernel,
        out_shape=jax.ShapeDtypeStruct(out_shape, jnp.bfloat16),
        in_specs=in_specs,
        out_specs=in_vmem(),
        scratch_shapes=scratch,
        compiler_params=pltpu.CompilerParams(vmem_limit_bytes=limit * 2**20),
        cost_estimate=pl.CostEstimate(flops=flops, bytes_accessed=2**22, transcendentals=0),
        name=name,
    )


def per_device(green, vertex):
    kx, ky = lax.axis_size("kx"), lax.axis_size("ky")
    groups = kx * ky
    rows, width, freqs = green.shape[1:]
    length = width * ky
    quad = length // groups
    bosons = vertex.shape[1]
    n = 2 * length
    dfts = jnp.asarray(tables(length, groups, kx))
    both = ("ky", "kx")

    block = green.reshape(2, ky, quad, width, freqs).transpose(1, 0, 2, 3, 4)
    block = lax.all_to_all(block, "ky", split_axis=0, concat_axis=0, tiled=True)
    spectrum = call(
        lambda *refs: columns_kernel(quad, groups, freqs, *refs),
        (n, quad * freqs),
        [in_vmem()] * 2,
        [pltpu.VMEM((quad * freqs // LANES, n, LANES), jnp.float32)],
        n * n * quad * freqs,
        16,
        "to_columns",
    )(block, dfts)
    spectrum = lax.all_to_all(spectrum, both, split_axis=0, concat_axis=0, tiled=True)
    field = call(
        lambda *refs: sites_kernel(quad, kx, freqs, bosons, *refs),
        (n, quad * freqs),
        [in_vmem()] * 3,
        [pltpu.VMEM((quad, 4, length // 2, freqs), jnp.bfloat16)] * 2
        + [pltpu.VMEM((2, bosons, freqs, freqs), jnp.bfloat16)],
        2 * n * n * quad * freqs + 6 * bosons * length * quad * freqs * freqs,
        24,
        "on_sites",
    )(spectrum, dfts, vertex)
    field = lax.all_to_all(field, both, split_axis=0, concat_axis=0, tiled=True)
    settled = call(
        lambda *refs: rows_kernel(quad, groups, freqs, *refs),
        (ky, 2, quad, width, freqs),
        [in_vmem()] * 2,
        [pltpu.VMEM((quad * freqs // LANES, n, LANES), jnp.float32), pltpu.VMEM((quad, n, freqs), jnp.bfloat16)],
        n * n * quad * freqs,
        16,
        "to_rows",
    )(field, dfts)
    settled = lax.all_to_all(settled, "ky", split_axis=0, concat_axis=0, tiled=True)
    return pl.pallas_call(
        lambda *refs: settle_kernel(ky, quad, *refs),
        out_shape=jax.ShapeDtypeStruct((2, rows, width, freqs), jnp.float32),
        in_specs=[in_vmem()],
        out_specs=pl.BlockSpec(memory_space=pltpu.HBM),
        scratch_shapes=[
            pltpu.VMEM((2, ky, quad, width, freqs), jnp.float32),
            pltpu.SemaphoreType.DMA((2, ky)),
        ],
        compiler_params=pltpu.CompilerParams(vmem_limit_bytes=12 * 2**20),
        name="to_output",
    )(settled)


def solution(mesh):
    placed = (P(None, "kx", "ky", None), P())
    return jax.shard_map(
        per_device, mesh=mesh, in_specs=placed, out_specs=P(None, "kx", "ky", None), check_vma=False
    )
```

```python
import math

import jax
import jax.numpy as jnp
import ml_dtypes
import numpy as np
from jax import lax
from jax.experimental import pallas as pl
from jax.experimental.pallas import tpu as pltpu
from jax.sharding import PartitionSpec as P

LANES = 128
TILE = 16
PIECES = 4
GROUP = 6


def pair_list(length):
    half = length // 2
    upper = (length - np.arange(half)) % length
    upper[0] = half
    return np.concatenate([np.arange(half), upper])


def complex_table(sites, momenta, length, direction, scale):
    phase = (sites[:, None].astype(np.int64) * momenta[None, :] % length) * (
        direction * 2.0 * math.pi / length
    )
    cos, sin = np.cos(phase) * scale, np.sin(phase) * scale
    return np.stack([np.stack([cos, -sin], 1), np.stack([sin, cos], 1)], 0)


def tables(length, groups, kx):
    quad = length // groups
    half = length // 2
    pairs = pair_list(length)
    low = np.arange(half)
    sent = low.reshape(kx // 2, groups // kx, quad).transpose(1, 0, 2).reshape(-1)
    own = np.stack([pairs[:half].reshape(groups, -1), pairs[half:].reshape(groups, -1)], 1).reshape(groups, quad)
    found = []
    for parity in range(2):
        y = own[:, parity::2].T.reshape(-1)
        x = np.concatenate([pairs[:half][parity::2], pairs[half:][parity::2]])
        cols = quad // 2
        t_y = complex_table(y, low, length, 1.0, 1.0)
        t_y = t_y.reshape(2, cols, groups, 2, half).transpose(1, 0, 2, 3, 4)
        t_x = complex_table(x, sent, length, 1.0, 1.0 / length).transpose(0, 1, 3, 2)
        b_x = complex_table(sent, x, length, -1.0, 1.0).transpose(1, 0, 2, 3)
        b_y = complex_table(low, y, length, -1.0, 1.0 / length)
        b_y = b_y.reshape(2, half, 2, cols, groups).transpose(0, 1, 3, 2, 4)
        found.append([t.reshape(length, length) for t in (t_y, t_x, b_x, b_y)])
    return np.stack([np.stack(f) for f in found], 1).astype(ml_dtypes.bfloat16)


def dot(left, right):
    return jnp.dot(left, right, preferred_element_type=jnp.float32)


def dot_turned(left, right):
    return lax.dot_general(left, right, (((1,), (1,)), ((), ())), preferred_element_type=jnp.float32)


def columns_kernel(quad, groups, freqs, block_ref, table_ref, out_ref, wide_ref):
    length = quad * groups

    def row(r, carry):
        both = [block_ref[:, c, r].reshape(length, freqs) for c in range(2)]
        low, high = [b[: length // 2] for b in both], [b[length // 2 :] for b in both]
        for parity in range(2):
            rhs = jnp.concatenate([a - b if parity else a + b for a, b in zip(low, high)], 0)
            product = dot(table_ref[0, parity], rhs)
            for at in range(quad):
                col, c = 2 * (at // 2) + parity, at % 2
                part = product[at * groups : (at + 1) * groups]
                for k in range(freqs // LANES):
                    spots = pl.ds(r * 2 + c, groups, stride=2 * quad)
                    wide_ref[col * (freqs // LANES) + k, spots, :] = part[:, k * LANES : (k + 1) * LANES]
        return carry

    for r in range(quad):
        row(r, 0)

    def settle(i, carry):
        at = pl.ds(pl.multiple_of(i * 128, 128), 128)
        for k in range(quad * freqs // LANES):
            out_ref[at, k * LANES : (k + 1) * LANES] = wide_ref[k, at, :].astype(jnp.bfloat16)
        return carry

    lax.fori_loop(0, 2 * length // 128, settle, 0, unroll=True)


def shifted(values, by):
    if by == 0:
        return values
    tail = jnp.zeros((values.shape[0], by), values.dtype)
    return jnp.concatenate([values[:, by:], tail], 1)


def swap_first(ref, col, c):
    low, high = ref[col, 2 * c, :TILE, :], ref[col, 2 * c + 1, :TILE, :]
    top = lax.broadcasted_iota(jnp.int32, low.shape, 0) == 0
    ref[col, 2 * c, :TILE, :] = jnp.where(top, high, low)
    ref[col, 2 * c + 1, :TILE, :] = jnp.where(top, low, high)


def sites_kernel(quad, kx, freqs, bosons, block_ref, table_ref, vertex_ref, out_ref, green_ref, field_ref, mixed_ref):
    half = green_ref.shape[2]
    length = 2 * half
    part = half // 2
    first = lax.axis_index("kx") + lax.axis_index("ky") == 0

    run = kx * quad
    sent = block_ref[...].reshape(length // run, 2, run, quad * freqs)
    low, high = [sent[:, i].reshape(length, quad * freqs) for i in range(2)]
    for parity in range(2):
        lattice = dot(table_ref[1, parity], low - high if parity else low + high).astype(jnp.bfloat16)
        for at in range(4):
            for col in range(quad):
                green_ref[col, at, parity * part : (parity + 1) * part, :] = lattice[
                    at * part : (at + 1) * part, col * freqs : (col + 1) * freqs
                ]
    for col in range(quad // 2, quad):
        for c in range(2):
            swap_first(green_ref, col, c)
    for w in range(bosons):
        v_re, v_im = vertex_ref[0, w], vertex_ref[1, w]
        mixed_ref[0, w] = v_im - v_re
        mixed_ref[1, w] = v_re + v_im

    def pair_block(step, carry):
        column, side = step // 2, step % 2
        alone = jnp.logical_and(first, column == 0)
        p_col = jnp.where(alone, side * (quad // 2), column)
        q_col = jnp.where(alone, side * (quad // 2), column + quad // 2)
        p_re, p_im = green_ref[p_col, side], green_ref[p_col, 2 + side]
        q_re, q_im = green_ref[q_col, 1 - side], green_ref[q_col, 3 - side]
        row = lax.broadcasted_iota(jnp.int32, (TILE, freqs), 0)
        own = jnp.logical_and(row == 0, alone)

        def mirror(mine, other):
            return jnp.concatenate([jnp.where(own, mine[:TILE], other[:TILE]), other[TILE:]], 0)

        totals = [jnp.zeros((half, freqs), jnp.float32) for _ in range(4)]
        for start in range(0, bosons, GROUP):
            sums = None
            for w in range(start, min(start + GROUP, bosons)):
                sp_re, sp_im = shifted(p_re, w), shifted(p_im, w)
                sq_re, sq_im = shifted(q_re, w), shifted(q_im, w)
                b_re, b_im = [], []
                for g_re, g_im, m_re, m_im in (
                    (p_re, p_im, mirror(sp_re, sq_re), mirror(sp_im, sq_im)),
                    (q_re, q_im, mirror(sq_re, sp_re), mirror(sq_im, sp_im)),
                ):
                    b_re.append(g_re * m_re - g_im * m_im)
                    b_im.append(g_re * m_im + g_im * m_re)
                b_re, b_im = jnp.concatenate(b_re, 0), jnp.concatenate(b_im, 0)
                if w % 2:
                    panel = jnp.concatenate([vertex_ref[0, w], vertex_ref[1, w]], 1)
                    c_re = dot_turned(jnp.concatenate([b_re, -b_im], 1), panel).astype(jnp.bfloat16)
                    c_im = dot_turned(jnp.concatenate([b_im, b_re], 1), panel).astype(jnp.bfloat16)
                else:
                    shared = dot_turned(b_re + b_im, vertex_ref[0, w])
                    c_re = (shared - dot_turned(b_im, mixed_ref[1, w])).astype(jnp.bfloat16)
                    c_im = (shared + dot_turned(b_re, mixed_ref[0, w])).astype(jnp.bfloat16)
                cp_re, cq_re, cp_im, cq_im = c_re[:half], c_re[half:], c_im[:half], c_im[half:]
                terms = [
                    sp_re * cp_re - sp_im * cp_im,
                    sp_re * cp_im + sp_im * cp_re,
                    sq_re * cq_re - sq_im * cq_im,
                    sq_re * cq_im + sq_im * cq_re,
                ]
                sums = terms if sums is None else [s + t for s, t in zip(sums, terms)]
            totals = [t + s.astype(jnp.float32) for t, s in zip(totals, sums)]
        p_sum_re, p_sum_im, q_sum_re, q_sum_im = [t.astype(jnp.bfloat16) for t in totals]
        field_ref[p_col, side] = p_sum_re
        field_ref[p_col, 2 + side] = p_sum_im
        field_ref[q_col, 1 - side] = q_sum_re
        field_ref[q_col, 3 - side] = q_sum_im
        return carry

    lax.fori_loop(0, quad, pair_block, 0)

    for col in range(quad // 2, quad):
        for c in range(2):
            swap_first(field_ref, col, c)
    for col in range(quad):
        lanes = slice(col * freqs, (col + 1) * freqs)
        even, odd = [
            dot(
                table_ref[2, parity],
                field_ref[col, :, parity * part : (parity + 1) * part, :].reshape(length, freqs),
            )
            for parity in range(2)
        ]
        for upper, total in ((0, even + odd), (1, even - odd)):
            total = total.astype(jnp.bfloat16)
            for k in range(length // run):
                at = (2 * k + upper) * run
                out_ref[at : at + run, lanes] = total[k * run : (k + 1) * run]


def rows_kernel(quad, groups, freqs, block_ref, table_ref, out_ref, wide_ref, rhs_ref):
    length = quad * groups
    targets, width = out_ref.shape[0], out_ref.shape[3]

    def widen(i, carry):
        at = pl.ds(pl.multiple_of(i * 128, 128), 128)
        for k in range(quad * freqs // LANES):
            wide_ref[k, at, :] = block_ref[at, k * LANES : (k + 1) * LANES].astype(jnp.float32)
        return carry

    lax.fori_loop(0, 2 * length // 128, widen, 0, unroll=True)

    def row(r, carry):
        for col in range(quad):
            for c in range(2):
                m = (col % 2) * length + ((col // 2) * 2 + c) * groups
                for k in range(freqs // LANES):
                    part = wide_ref[col * (freqs // LANES) + k, pl.ds(r * 2 + c, groups, stride=2 * quad), :]
                    rhs_ref[r, m : m + groups, k * LANES : (k + 1) * LANES] = part.astype(jnp.bfloat16)
        even, odd = [
            dot(table_ref[3, parity], rhs_ref[r, parity * length : (parity + 1) * length, :]) for parity in range(2)
        ]
        for upper, total in ((0, even + odd), (1, even - odd)):
            total = total.astype(jnp.bfloat16)
            for c in range(2):
                part = total[c * (length // 2) : (c + 1) * (length // 2)]
                out_ref[upper * (targets // 2) : (upper + 1) * (targets // 2), c, r] = part.reshape(
                    targets // 2, width, freqs
                )
        return carry

    for r in range(quad):
        row(r, 0)


def settle_kernel(devices, block_ref, out_hbm, wide_ref, sems):
    few = devices // PIECES
    copies = []
    for c in range(2):
        for i in range(PIECES):
            for d in range(i * few, (i + 1) * few):
                wide_ref[c, d] = block_ref[d, c].astype(jnp.float32)
            at = pl.ds(i * few, few)
            copy = pltpu.make_async_copy(wide_ref.at[c, at], out_hbm.at[c, at], sems.at[c, i])
            copy.start()
            copies.append(copy)
    for copy in copies:
        copy.wait()


def in_vmem():
    return pl.BlockSpec(memory_space=pltpu.VMEM)


def call(kernel, out_shape, in_specs, scratch, flops, limit, name):
    return pl.pallas_call(
        kernel,
        out_shape=jax.ShapeDtypeStruct(out_shape, jnp.bfloat16),
        in_specs=in_specs,
        out_specs=in_vmem(),
        scratch_shapes=scratch,
        compiler_params=pltpu.CompilerParams(vmem_limit_bytes=limit * 2**20),
        cost_estimate=pl.CostEstimate(flops=flops, bytes_accessed=2**22, transcendentals=0),
        name=name,
    )


def per_device(green, vertex):
    kx, ky = lax.axis_size("kx"), lax.axis_size("ky")
    groups = kx * ky
    rows, width, freqs = green.shape[1:]
    length = width * ky
    quad = length // groups
    bosons = vertex.shape[1]
    n = 2 * length
    dfts = jnp.asarray(tables(length, groups, kx))
    both = ("ky", "kx")

    block = green.reshape(2, ky, quad, width, freqs).transpose(1, 0, 2, 3, 4)
    block = lax.all_to_all(block, "ky", split_axis=0, concat_axis=0, tiled=True)
    spectrum = call(
        lambda *refs: columns_kernel(quad, groups, freqs, *refs),
        (n, quad * freqs),
        [in_vmem()] * 2,
        [pltpu.VMEM((quad * freqs // LANES, n, LANES), jnp.float32)],
        n * n * quad * freqs,
        16,
        "to_columns",
    )(block, dfts)
    spectrum = lax.all_to_all(spectrum, both, split_axis=0, concat_axis=0, tiled=True)
    field = call(
        lambda *refs: sites_kernel(quad, kx, freqs, bosons, *refs),
        (n, quad * freqs),
        [in_vmem()] * 3,
        [pltpu.VMEM((quad, 4, length // 2, freqs), jnp.bfloat16)] * 2
        + [pltpu.VMEM((2, bosons, freqs, freqs), jnp.bfloat16)],
        2 * n * n * quad * freqs + 6 * bosons * length * quad * freqs * freqs,
        24,
        "on_sites",
    )(spectrum, dfts, vertex)
    field = lax.all_to_all(field, both, split_axis=0, concat_axis=0, tiled=True)
    settled = call(
        lambda *refs: rows_kernel(quad, groups, freqs, *refs),
        (ky, 2, quad, width, freqs),
        [in_vmem()] * 2,
        [pltpu.VMEM((quad * freqs // LANES, n, LANES), jnp.float32), pltpu.VMEM((quad, n, freqs), jnp.bfloat16)],
        n * n * quad * freqs,
        16,
        "to_rows",
    )(field, dfts)
    settled = lax.all_to_all(settled, "ky", split_axis=0, concat_axis=0, tiled=True)
    return pl.pallas_call(
        lambda *refs: settle_kernel(ky, *refs),
        out_shape=jax.ShapeDtypeStruct((2, ky, quad, width, freqs), jnp.float32),
        in_specs=[in_vmem()],
        out_specs=pl.BlockSpec(memory_space=pltpu.HBM),
        scratch_shapes=[
            pltpu.VMEM((2, ky, quad, width, freqs), jnp.float32),
            pltpu.SemaphoreType.DMA((2, PIECES)),
        ],
        compiler_params=pltpu.CompilerParams(vmem_limit_bytes=12 * 2**20),
        name="to_output",
    )(settled).reshape(2, rows, width, freqs)


def solution(mesh):
    placed = (P(None, "kx", "ky", None), P())
    return jax.shard_map(
        per_device, mesh=mesh, in_specs=placed, out_specs=P(None, "kx", "ky", None), check_vma=False
    )
```

```python
import math

import jax
import jax.numpy as jnp
import ml_dtypes
import numpy as np
from jax import lax
from jax.experimental import pallas as pl
from jax.experimental.pallas import tpu as pltpu
from jax.sharding import PartitionSpec as P

LANES = 128
TILE = 16
PIECES = 2
GROUP = 6


def pair_list(length):
    half = length // 2
    upper = (length - np.arange(half)) % length
    upper[0] = half
    return np.concatenate([np.arange(half), upper])


def complex_table(sites, momenta, length, direction, scale):
    phase = (sites[:, None].astype(np.int64) * momenta[None, :] % length) * (
        direction * 2.0 * math.pi / length
    )
    cos, sin = np.cos(phase) * scale, np.sin(phase) * scale
    return np.stack([np.stack([cos, -sin], 1), np.stack([sin, cos], 1)], 0)


def tables(length, groups, kx):
    quad = length // groups
    half = length // 2
    pairs = pair_list(length)
    low = np.arange(half)
    sent = low.reshape(kx // 2, groups // kx, quad).transpose(1, 0, 2).reshape(-1)
    own = np.stack([pairs[:half].reshape(groups, -1), pairs[half:].reshape(groups, -1)], 1).reshape(groups, quad)
    found = []
    for parity in range(2):
        y = own[:, parity::2].T.reshape(-1)
        x = np.concatenate([pairs[:half][parity::2], pairs[half:][parity::2]])
        cols = quad // 2
        t_y = complex_table(y, low, length, 1.0, 1.0)
        t_y = t_y.reshape(2, cols, groups, 2, half).transpose(1, 0, 2, 3, 4)
        t_x = complex_table(x, sent, length, 1.0, 1.0 / length).transpose(0, 1, 3, 2)
        b_x = complex_table(sent, x, length, -1.0, 1.0).transpose(1, 0, 2, 3)
        b_y = complex_table(low, y, length, -1.0, 1.0 / length)
        b_y = b_y.reshape(2, half, 2, cols, groups).transpose(0, 1, 3, 2, 4)
        found.append([t.reshape(length, length) for t in (t_y, t_x, b_x, b_y)])
    return np.stack([np.stack(f) for f in found], 1).astype(ml_dtypes.bfloat16)


def dot(left, right):
    return jnp.dot(left, right, preferred_element_type=jnp.float32)


def dot_turned(left, right):
    return lax.dot_general(left, right, (((1,), (1,)), ((), ())), preferred_element_type=jnp.float32)


def columns_kernel(quad, groups, freqs, block_ref, table_ref, out_ref, wide_ref):
    length = quad * groups

    def row(r, carry):
        both = [block_ref[:, c, r].reshape(length, freqs) for c in range(2)]
        low, high = [b[: length // 2] for b in both], [b[length // 2 :] for b in both]
        for parity in range(2):
            rhs = jnp.concatenate([a - b if parity else a + b for a, b in zip(low, high)], 0)
            product = dot(table_ref[0, parity], rhs)
            for at in range(quad):
                col, c = 2 * (at // 2) + parity, at % 2
                part = product[at * groups : (at + 1) * groups]
                for k in range(freqs // LANES):
                    spots = pl.ds(r * 2 + c, groups, stride=2 * quad)
                    wide_ref[col * (freqs // LANES) + k, spots, :] = part[:, k * LANES : (k + 1) * LANES]
        return carry

    for r in range(quad):
        row(r, 0)

    def settle(i, carry):
        at = pl.ds(pl.multiple_of(i * 128, 128), 128)
        for k in range(quad * freqs // LANES):
            out_ref[at, k * LANES : (k + 1) * LANES] = wide_ref[k, at, :].astype(jnp.bfloat16)
        return carry

    lax.fori_loop(0, 2 * length // 128, settle, 0, unroll=True)


def shifted(values, by):
    if by == 0:
        return values
    tail = jnp.zeros((values.shape[0], by), values.dtype)
    return jnp.concatenate([values[:, by:], tail], 1)


def swap_first(ref, col, c):
    low, high = ref[col, 2 * c, :TILE, :], ref[col, 2 * c + 1, :TILE, :]
    top = lax.broadcasted_iota(jnp.int32, low.shape, 0) == 0
    ref[col, 2 * c, :TILE, :] = jnp.where(top, high, low)
    ref[col, 2 * c + 1, :TILE, :] = jnp.where(top, low, high)


def sites_kernel(quad, kx, freqs, bosons, block_ref, table_ref, vertex_ref, out_ref, green_ref, field_ref, mixed_ref):
    half = green_ref.shape[2]
    length = 2 * half
    part = half // 2
    first = lax.axis_index("kx") + lax.axis_index("ky") == 0

    run = kx * quad
    sent = block_ref[...].reshape(length // run, 2, run, quad * freqs)
    low, high = [sent[:, i].reshape(length, quad * freqs) for i in range(2)]
    for parity in range(2):
        lattice = dot(table_ref[1, parity], low - high if parity else low + high).astype(jnp.bfloat16)
        for at in range(4):
            for col in range(quad):
                green_ref[col, at, parity * part : (parity + 1) * part, :] = lattice[
                    at * part : (at + 1) * part, col * freqs : (col + 1) * freqs
                ]
    for col in range(quad // 2, quad):
        for c in range(2):
            swap_first(green_ref, col, c)
    for w in range(bosons):
        v_re, v_im = vertex_ref[0, w], vertex_ref[1, w]
        mixed_ref[0, w] = v_im - v_re
        mixed_ref[1, w] = v_re + v_im

    def pair_block(step, carry):
        column, side = step // 2, step % 2
        alone = jnp.logical_and(first, column == 0)
        p_col = jnp.where(alone, side * (quad // 2), column)
        q_col = jnp.where(alone, side * (quad // 2), column + quad // 2)
        p_re, p_im = green_ref[p_col, side], green_ref[p_col, 2 + side]
        q_re, q_im = green_ref[q_col, 1 - side], green_ref[q_col, 3 - side]
        row = lax.broadcasted_iota(jnp.int32, (TILE, freqs), 0)
        own = jnp.logical_and(row == 0, alone)

        def mirror(mine, other):
            return jnp.concatenate([jnp.where(own, mine[:TILE], other[:TILE]), other[TILE:]], 0)

        totals = [jnp.zeros((half, freqs), jnp.float32) for _ in range(4)]
        for start in range(0, bosons, GROUP):
            sums = None
            for w in range(start, min(start + GROUP, bosons)):
                sp_re, sp_im = shifted(p_re, w), shifted(p_im, w)
                sq_re, sq_im = shifted(q_re, w), shifted(q_im, w)
                b_re, b_im = [], []
                for g_re, g_im, m_re, m_im in (
                    (p_re, p_im, mirror(sp_re, sq_re), mirror(sp_im, sq_im)),
                    (q_re, q_im, mirror(sq_re, sp_re), mirror(sq_im, sp_im)),
                ):
                    b_re.append(g_re * m_re - g_im * m_im)
                    b_im.append(g_re * m_im + g_im * m_re)
                b_re, b_im = jnp.concatenate(b_re, 0), jnp.concatenate(b_im, 0)
                if w % 2:
                    panel = jnp.concatenate([vertex_ref[0, w], vertex_ref[1, w]], 1)
                    c_re = dot_turned(jnp.concatenate([b_re, -b_im], 1), panel).astype(jnp.bfloat16)
                    c_im = dot_turned(jnp.concatenate([b_im, b_re], 1), panel).astype(jnp.bfloat16)
                else:
                    shared = dot_turned(b_re + b_im, vertex_ref[0, w])
                    c_re = (shared - dot_turned(b_im, mixed_ref[1, w])).astype(jnp.bfloat16)
                    c_im = (shared + dot_turned(b_re, mixed_ref[0, w])).astype(jnp.bfloat16)
                cp_re, cq_re, cp_im, cq_im = c_re[:half], c_re[half:], c_im[:half], c_im[half:]
                terms = [
                    sp_re * cp_re - sp_im * cp_im,
                    sp_re * cp_im + sp_im * cp_re,
                    sq_re * cq_re - sq_im * cq_im,
                    sq_re * cq_im + sq_im * cq_re,
                ]
                sums = terms if sums is None else [s + t for s, t in zip(sums, terms)]
            totals = [t + s.astype(jnp.float32) for t, s in zip(totals, sums)]
        p_sum_re, p_sum_im, q_sum_re, q_sum_im = [t.astype(jnp.bfloat16) for t in totals]
        field_ref[p_col, side] = p_sum_re
        field_ref[p_col, 2 + side] = p_sum_im
        field_ref[q_col, 1 - side] = q_sum_re
        field_ref[q_col, 3 - side] = q_sum_im
        return carry

    lax.fori_loop(0, quad, pair_block, 0)

    for col in range(quad // 2, quad):
        for c in range(2):
            swap_first(field_ref, col, c)
    for col in range(quad):
        lanes = slice(col * freqs, (col + 1) * freqs)
        even, odd = [
            dot(
                table_ref[2, parity],
                field_ref[col, :, parity * part : (parity + 1) * part, :].reshape(length, freqs),
            )
            for parity in range(2)
        ]
        for upper, total in ((0, even + odd), (1, even - odd)):
            total = total.astype(jnp.bfloat16)
            for k in range(length // run):
                at = (2 * k + upper) * run
                out_ref[at : at + run, lanes] = total[k * run : (k + 1) * run]


def rows_kernel(quad, groups, freqs, block_ref, table_ref, out_ref, wide_ref, rhs_ref):
    length = quad * groups
    targets, width = out_ref.shape[0], out_ref.shape[3]

    def widen(i, carry):
        at = pl.ds(pl.multiple_of(i * 128, 128), 128)
        for k in range(quad * freqs // LANES):
            wide_ref[k, at, :] = block_ref[at, k * LANES : (k + 1) * LANES].astype(jnp.float32)
        return carry

    lax.fori_loop(0, 2 * length // 128, widen, 0, unroll=True)

    def row(r, carry):
        for col in range(quad):
            for c in range(2):
                m = (col % 2) * length + ((col // 2) * 2 + c) * groups
                for k in range(freqs // LANES):
                    part = wide_ref[col * (freqs // LANES) + k, pl.ds(r * 2 + c, groups, stride=2 * quad), :]
                    rhs_ref[r, m : m + groups, k * LANES : (k + 1) * LANES] = part.astype(jnp.bfloat16)
        even, odd = [
            dot(table_ref[3, parity], rhs_ref[r, parity * length : (parity + 1) * length, :]) for parity in range(2)
        ]
        for upper, total in ((0, even + odd), (1, even - odd)):
            total = total.astype(jnp.bfloat16)
            for c in range(2):
                part = total[c * (length // 2) : (c + 1) * (length // 2)]
                out_ref[upper * (targets // 2) : (upper + 1) * (targets // 2), c, r] = part.reshape(
                    targets // 2, width, freqs
                )
        return carry

    for r in range(quad):
        row(r, 0)


def settle_kernel(devices, block_ref, out_hbm, wide_ref, sems):
    few = devices // PIECES
    copies = []
    for c in range(2):
        for i in range(PIECES):
            for d in range(i * few, (i + 1) * few):
                wide_ref[c, d] = block_ref[d, c].astype(jnp.float32)
            at = pl.ds(i * few, few)
            copy = pltpu.make_async_copy(wide_ref.at[c, at], out_hbm.at[c, at], sems.at[c, i])
            copy.start()
            copies.append(copy)
    for copy in copies:
        copy.wait()


def in_vmem():
    return pl.BlockSpec(memory_space=pltpu.VMEM)


def call(kernel, out_shape, in_specs, scratch, flops, limit, name):
    return pl.pallas_call(
        kernel,
        out_shape=jax.ShapeDtypeStruct(out_shape, jnp.bfloat16),
        in_specs=in_specs,
        out_specs=in_vmem(),
        scratch_shapes=scratch,
        compiler_params=pltpu.CompilerParams(vmem_limit_bytes=limit * 2**20),
        cost_estimate=pl.CostEstimate(flops=flops, bytes_accessed=2**22, transcendentals=0),
        name=name,
    )


def per_device(green, vertex):
    kx, ky = lax.axis_size("kx"), lax.axis_size("ky")
    groups = kx * ky
    rows, width, freqs = green.shape[1:]
    length = width * ky
    quad = length // groups
    bosons = vertex.shape[1]
    n = 2 * length
    dfts = jnp.asarray(tables(length, groups, kx))
    both = ("ky", "kx")

    block = green.reshape(2, ky, quad, width, freqs).transpose(1, 0, 2, 3, 4)
    block = lax.all_to_all(block, "ky", split_axis=0, concat_axis=0, tiled=True)
    spectrum = call(
        lambda *refs: columns_kernel(quad, groups, freqs, *refs),
        (n, quad * freqs),
        [in_vmem()] * 2,
        [pltpu.VMEM((quad * freqs // LANES, n, LANES), jnp.float32)],
        n * n * quad * freqs,
        16,
        "to_columns",
    )(block, dfts)
    spectrum = lax.all_to_all(spectrum, both, split_axis=0, concat_axis=0, tiled=True)
    field = call(
        lambda *refs: sites_kernel(quad, kx, freqs, bosons, *refs),
        (n, quad * freqs),
        [in_vmem()] * 3,
        [pltpu.VMEM((quad, 4, length // 2, freqs), jnp.bfloat16)] * 2
        + [pltpu.VMEM((2, bosons, freqs, freqs), jnp.bfloat16)],
        2 * n * n * quad * freqs + 6 * bosons * length * quad * freqs * freqs,
        24,
        "on_sites",
    )(spectrum, dfts, vertex)
    field = lax.all_to_all(field, both, split_axis=0, concat_axis=0, tiled=True)
    settled = call(
        lambda *refs: rows_kernel(quad, groups, freqs, *refs),
        (ky, 2, quad, width, freqs),
        [in_vmem()] * 2,
        [pltpu.VMEM((quad * freqs // LANES, n, LANES), jnp.float32), pltpu.VMEM((quad, n, freqs), jnp.bfloat16)],
        n * n * quad * freqs,
        16,
        "to_rows",
    )(field, dfts)
    settled = lax.all_to_all(settled, "ky", split_axis=0, concat_axis=0, tiled=True)
    return pl.pallas_call(
        lambda *refs: settle_kernel(ky, *refs),
        out_shape=jax.ShapeDtypeStruct((2, ky, quad, width, freqs), jnp.float32),
        in_specs=[in_vmem()],
        out_specs=pl.BlockSpec(memory_space=pltpu.HBM),
        scratch_shapes=[
            pltpu.VMEM((2, ky, quad, width, freqs), jnp.float32),
            pltpu.SemaphoreType.DMA((2, PIECES)),
        ],
        compiler_params=pltpu.CompilerParams(vmem_limit_bytes=12 * 2**20),
        name="to_output",
    )(settled).reshape(2, rows, width, freqs)


def solution(mesh):
    placed = (P(None, "kx", "ky", None), P())
    return jax.shard_map(
        per_device, mesh=mesh, in_specs=placed, out_specs=P(None, "kx", "ky", None), check_vma=False
    )
```
